128 devices in a mesh: row: 8 (over y, z_lo), col: 16 (over x, z_hi, core).
Axes of the slice: x: 4, y: 4, z: 4 (z_hi: 2, z_lo: 2; z = z_hi * 2 + z_lo), core: 2. Of those that a mesh axis runs over, the one named last changes fastest.
Arguments:
- projections: float32 [24576, 256], P(('row', 'col')), may hold values from -1.5 to 1.5
- partner: int32 [24576], P(('row', 'col')), may hold values from 0 to 24575, as said below
Outputs:
- mean_objective: float32 [], replicated
- grad_projections: float32 [24576, 256], P(('row', 'col'))
The draws below stay inside these ranges and needn't reach their ends.
Inputs may be any that keep to these rules, and one draw needn't show every extreme that they name: partner pairs the views: partner[partner[i]] == i and partner[i] != i for every view i.
All inputs are finite; a program needn't handle non-finite values.
Results may differ from the reference program's by a relative error of at most 0.0003.
Values sent between devices are 32-bit elements; how exact they have to be, the bound alone decides.
No kernel may reach another device: no remote copies, remote signals or barrier semaphores. Data moves between devices by JAX's collectives and lax.ppermute only.
A program may use at most 128 MiB of HBM per device.

```python
import math
import jax
import jax.numpy as jnp
from jax import lax

D = 256
VIEWS = 24576


def pair_order(key):
    return jax.random.permutation(jax.random.fold_in(key, 101), VIEWS).astype(jnp.int32)


def draw_partner(key, part):
    order = pair_order(key)
    first = order[0::2]
    second = order[1::2]
    base = jnp.zeros((VIEWS,), jnp.int32)
    return base.at[first].set(second).at[second].set(first)


def draw_projections(key, part):
    order = pair_order(key)
    key = jax.random.fold_in(key, 23)
    images = VIEWS // 2
    classes = (images + 31) // 32
    picture = jnp.zeros((VIEWS,), jnp.int32).at[order].set(jnp.arange(VIEWS, dtype=jnp.int32) // 2)
    family = picture // 32
    subkeys = jax.random.split(key, 7)
    root = 1.0 / math.sqrt(D)
    centre = jax.random.truncated_normal(subkeys[0], -3.0, 3.0, (classes, D), jnp.float32) * root
    itself = jax.random.truncated_normal(subkeys[1], -3.0, 3.0, (images, D), jnp.float32) * root
    jitter = jax.random.truncated_normal(subkeys[2], -3.0, 3.0, (VIEWS, D), jnp.float32) * root
    tightness = jax.random.uniform(subkeys[3], (classes,), jnp.float32, 0.5, 0.85)
    spread = jax.random.uniform(subkeys[4], (images,), jnp.float32, 0.2, 0.3)
    position = (jnp.arange(VIEWS, dtype=jnp.float32) + 0.5) / VIEWS
    blurring = (0.05 + position) * jax.random.uniform(subkeys[5], (VIEWS,), jnp.float32, 0.6, 1.4)
    vectors = jnp.sqrt(tightness)[family][:, None] * centre[family]
    vectors = vectors + jnp.sqrt(spread)[picture][:, None] * itself[picture]
    vectors = vectors + jnp.sqrt(blurring)[:, None] * jitter
    lengths = jnp.exp(jax.random.uniform(subkeys[6], (VIEWS, 1), jnp.float32, math.log(0.5), math.log(8.0)))
    return jnp.clip(vectors * lengths, -1.5, 1.5)


def setup_inputs(seed: int = 0) -> dict:
    keys = jax.random.split(jax.random.key(seed), 3)
    return {
        "projections": draw_projections(jax.random.fold_in(keys[2], 71), 0),
        "partner": draw_partner(jax.random.fold_in(keys[2], 71), 0),
    }


logit_divisor = 0.1

def normalize(rows):
    scale = lax.rsqrt(lax.optimization_barrier(jnp.sum(rows * rows, axis=-1, keepdims=True)) + 1e-06)
    return (rows * scale, scale)

def scores_of(source_tile, target_tile):
    return lax.dot_general(source_tile, target_tile, (((1,), (1,)), ((), ())), precision=lax.Precision.HIGHEST, preferred_element_type=jnp.float32) / logit_divisor

def reference(projections, partner):
    z, scale = normalize(projections)
    overall_aggregate = z.shape[0]
    tile_span_length = z.shape[1]
    block = 1024 if overall_aggregate % 1024 == 0 else overall_aggregate
    view_tally = overall_aggregate // block
    view_positions = jnp.arange(overall_aggregate, dtype=jnp.int32)
    embedding_tiles = z.reshape(view_tally, block, tile_span_length)
    partner_tiles = partner.reshape(view_tally, block)
    anchor_tiles = view_positions.reshape(view_tally, block)

    def expo(z_blk, anchor_tile_number):
        cosine_matrix = scores_of(z_blk, z)
        exponentiated_logits = jnp.where(view_positions[None, :] == anchor_tile_number[:, None], jnp.float32(0.0), jnp.exp(cosine_matrix - 1.0 / logit_divisor))
        return (cosine_matrix, exponentiated_logits)

    def stats(args):
        z_blk, p_blk, anchor_tile_number = args
        cosine_matrix, exponentiated_logits = expo(z_blk, anchor_tile_number)
        anchor_partition_value = lax.optimization_barrier(jnp.sum(exponentiated_logits, axis=1))
        partner_logit = lax.optimization_barrier(jnp.sum(jnp.where(view_positions[None, :] == p_blk[:, None], cosine_matrix, jnp.float32(0.0)), axis=1))
        return (anchor_partition_value, partner_logit)
    anchor_partition_value, partner_logit = lax.map(stats, (embedding_tiles, partner_tiles, anchor_tiles))
    mean_objective = jnp.mean(jnp.log(anchor_partition_value) + 1.0 / logit_divisor - partner_logit)

    def derivative_list(carry, args):
        z_blk, p_blk, anchor_tile_number, r_blk = args
        cosine_matrix, exponentiated_logits = expo(z_blk, anchor_tile_number)
        g = exponentiated_logits / r_blk[:, None] - jnp.where(view_positions[None, :] == p_blk[:, None], jnp.float32(1.0), jnp.float32(0.0))
        a_blk = jnp.dot(g, z, precision=lax.Precision.HIGHEST, preferred_element_type=jnp.float32)
        carry = carry + lax.dot_general(g, z_blk, (((0,), (0,)), ((), ())), precision=lax.Precision.HIGHEST, preferred_element_type=jnp.float32)
        return (carry, a_blk)
    offset_first = jnp.zeros((overall_aggregate, tile_span_length), jnp.float32)
    target_contributions, source_contributions = lax.scan(derivative_list, offset_first, (embedding_tiles, partner_tiles, anchor_tiles, anchor_partition_value))
    embedding_derivative = (source_contributions.reshape(overall_aggregate, tile_span_length) + target_contributions) / logit_divisor
    grad = (embedding_derivative - z * lax.optimization_barrier(jnp.sum(z * embedding_derivative, axis=-1, keepdims=True))) * scale
    return (mean_objective, grad)
```

```python
import functools

import jax
import jax.numpy as jnp
from jax import lax
from jax.experimental import pallas as pl
from jax.experimental.pallas import tpu as pltpu
from jax.sharding import Mesh, PartitionSpec as P

f32, bf16 = jnp.float32, jnp.bfloat16
PER = 192
D = 256
VIEWS = 24576
C_BLOCKS = 8
R_BLOCKS = 16
C = C_BLOCKS * PER
R = R_BLOCKS * PER
SPAN = 768
STEPS = R // SPAN
LANES = 256
BLOCK = 200
TEMPERATURE = 0.1
LOG2E = 1.4426950408889634
LN2 = 0.6931471805599453
NT = (((1,), (1,)), ((), ()))
ROW = ("y", "zl")
COL = ("x", "zh", "core")
ALL = ROW + COL


def unit(rows):
    return rows * lax.rsqrt(jnp.sum(rows * rows, axis=-1, keepdims=True) + 1e-06)


def halves(a):
    hi = a.astype(bf16)
    return hi, (a - hi.astype(f32)).astype(bf16)


def score_kernel(
    first_ref, xc_ref, own_ref, other_ref, ids_ref, partner_ref,
    e_ref, zr_ref, rsum_ref, csum_ref, pos_ref, cid_ref,
    a_ref, b_ref, cacc_ref, pacc_ref,
):
    k = pl.program_id(0)
    nb = SPAN // PER

    @pl.when(k == 0)
    def _():
        cacc_ref[...] = jnp.zeros_like(cacc_ref)
        pacc_ref[...] = jnp.zeros_like(pacc_ref)

        @pl.loop(0, C_BLOCKS)
        def _(b):
            rows = pl.ds(pl.multiple_of(b * PER, PER), PER)
            hi, lo = halves(unit(xc_ref[b]) * (LOG2E / TEMPERATURE))
            a_ref[rows, 0:D] = hi
            a_ref[rows, D : 2 * D] = lo
            a_ref[rows, 2 * D : 3 * D] = hi
            cid_ref[rows, :] = (
                first_ref[0] + b * (R_BLOCKS * PER) + lax.broadcasted_iota(jnp.int32, (PER, 128), 0)
            )

    def prepare(blocks_ref):
        for b in range(nb):
            hi, lo = halves(unit(blocks_ref[b, 0:PER, :]))
            rows = pl.ds(b * PER, PER)
            b_ref[rows, 0:D] = hi
            b_ref[rows, D : 2 * D] = hi
            b_ref[rows, 2 * D : 3 * D] = lo
            zr_ref[rows, 0:D] = hi
            zr_ref[rows, D : 2 * D] = lo

    @pl.when(k < STEPS // 2)
    def _():
        prepare(own_ref)

    @pl.when(k >= STEPS // 2)
    def _():
        prepare(other_ref)

    cid = cid_ref[...]
    for n in range(SPAN // LANES):
        cols = pl.ds(n * LANES, LANES)
        s = lax.dot_general(a_ref[...], b_ref[cols, :], NT, preferred_element_type=f32)
        row_total = None
        for h in range(LANES // 128):
            lanes = pl.ds(n * LANES + h * 128, 128)
            part = s[:, h * 128 : (h + 1) * 128]
            e = jnp.where(cid == ids_ref[:, lanes], 0.0, jnp.exp2(part))
            hit = jnp.where(cid == partner_ref[:, lanes], part, 0.0)
            e_ref[:, lanes] = e
            rsum_ref[:, lanes] = jnp.sum(e, axis=0, keepdims=True)
            pacc_ref[...] += jnp.sum(hit.reshape(C // 8, 8, 128), axis=0)
            row_total = e if row_total is None else row_total + e
        cacc_ref[...] += row_total

    @pl.when(k == STEPS - 1)
    def _():
        csum_ref[...] = lax.dot_general(
            jnp.ones((8, 128), f32), cacc_ref[...], NT, precision=lax.Precision.HIGHEST, preferred_element_type=f32
        )
        pos_ref[...] = pacc_ref[...]


def scores(first, xc, own, other, ids, partner):
    half = STEPS // 2
    nb = SPAN // PER
    whole = lambda k: (0, 0)
    return pl.pallas_call(
        score_kernel,
        grid=(STEPS,),
        in_specs=[
            pl.BlockSpec(memory_space=pltpu.SMEM),
            pl.BlockSpec((C_BLOCKS, PER, D), lambda k: (0, 0, 0)),
            pl.BlockSpec((nb, BLOCK, D), lambda k: (jnp.minimum(k, half - 1), 0, 0)),
            pl.BlockSpec((nb, BLOCK, D), lambda k: (jnp.maximum(k - half, 0), 0, 0)),
            pl.BlockSpec((1, SPAN), lambda k: (0, k)),
            pl.BlockSpec((1, SPAN), lambda k: (0, k)),
        ],
        out_specs=[
            pl.BlockSpec((C, SPAN), lambda k: (0, k)),
            pl.BlockSpec((SPAN, 2 * D), lambda k: (k, 0)),
            pl.BlockSpec((1, SPAN), lambda k: (0, k)),
            pl.BlockSpec((8, C), whole),
            pl.BlockSpec((8, 128), whole),
            pl.BlockSpec((C, 128), whole),
        ],
        out_shape=[
            jax.ShapeDtypeStruct((C, R), f32),
            jax.ShapeDtypeStruct((R, 2 * D), bf16),
            jax.ShapeDtypeStruct((1, R), f32),
            jax.ShapeDtypeStruct((8, C), f32),
            jax.ShapeDtypeStruct((8, 128), f32),
            jax.ShapeDtypeStruct((C, 128), jnp.int32),
        ],
        scratch_shapes=[
            pltpu.VMEM((C, 3 * D), bf16),
            pltpu.VMEM((SPAN, 3 * D), bf16),
            pltpu.VMEM((C, 128), f32),
            pltpu.VMEM((8, 128), f32),
        ],
        compiler_params=pltpu.CompilerParams(vmem_limit_bytes=56 << 20),
    )(first, xc, own, other, ids, partner)


def gradient_kernel(
    logs_ref, e_ref, z_ref, ur_ref, uc_ref, partner_ref, cid_ref,
    out_ref,
    g_ref, w_ref, acc_ref,
):
    k = pl.program_id(0)

    @pl.when(k == 0)
    def _():
        acc_ref[...] = jnp.zeros_like(acc_ref)

    w_ref[0:SPAN, :] = z_ref[:, 0:D]
    w_ref[SPAN : 2 * SPAN, :] = z_ref[:, 0:D]
    w_ref[2 * SPAN : 3 * SPAN, :] = z_ref[:, D : 2 * D]
    for h in range(SPAN // 128):
        lanes = pl.ds(h * 128, 128)
        g = e_ref[:, lanes] * (uc_ref[...] + ur_ref[:, lanes])
        g = g - jnp.where(cid_ref[...] == partner_ref[:, lanes], 2.0, 0.0)
        hi, lo = halves(g)
        g_ref[:, lanes] = hi
        g_ref[:, pl.ds(SPAN + h * 128, 128)] = lo
        g_ref[:, pl.ds(2 * SPAN + h * 128, 128)] = hi
    acc_ref[...] += jnp.dot(g_ref[...], w_ref[...], preferred_element_type=f32)

    @pl.when(k == STEPS - 1)
    def _():
        for b in range(C_BLOCKS):
            out_ref[b, 0:PER, :] = acc_ref[b * PER : (b + 1) * PER, :]
            out_ref[b, PER:BLOCK, :] = jnp.full((BLOCK - PER, D), logs_ref[0], f32)


def gradients(logs, e, z, ur, uc, partner, cid):
    whole = lambda k: (0, 0)
    return pl.pallas_call(
        gradient_kernel,
        grid=(STEPS,),
        in_specs=[
            pl.BlockSpec(memory_space=pltpu.SMEM),
            pl.BlockSpec((C, SPAN), lambda k: (0, k)),
            pl.BlockSpec((SPAN, 2 * D), lambda k: (k, 0)),
            pl.BlockSpec((1, SPAN), lambda k: (0, k)),
            pl.BlockSpec((C, 128), whole),
            pl.BlockSpec((1, SPAN), lambda k: (0, k)),
            pl.BlockSpec((C, 128), whole),
        ],
        out_specs=pl.BlockSpec((C_BLOCKS, BLOCK, D), lambda k: (0, 0, 0)),
        out_shape=jax.ShapeDtypeStruct((C_BLOCKS, BLOCK, D), f32),
        scratch_shapes=[
            pltpu.VMEM((C, 3 * SPAN), bf16),
            pltpu.VMEM((3 * SPAN, D), bf16),
            pltpu.VMEM((C, D), f32),
        ],
        compiler_params=pltpu.CompilerParams(vmem_limit_bytes=60 << 20),
    )(logs, e, z, ur, uc, partner, cid)


def by_core(pair, core):
    return jnp.where(core == 0, pair, pair[::-1])


def shards(projections, partner):
    row = lax.axis_index(ROW)
    col = lax.axis_index(COL)
    core = lax.axis_index("core")

    xc = jnp.broadcast_to(projections[None], (C_BLOCKS, PER, D)).reshape(C, D)
    xc = lax.all_to_all(xc, ROW, 0, 0, tiled=True).reshape(C_BLOCKS, PER, D)
    tail = jnp.pad(partner.astype(f32)[None], ((0, BLOCK - PER - 1), (0, D - PER)))
    block = jnp.concatenate([projections, tail])
    own = jnp.broadcast_to(block[None], (8, BLOCK, D)).reshape(8 * BLOCK, D)
    own = lax.all_to_all(own, ("x", "zh"), 0, 0, tiled=True)
    other = lax.ppermute(own, "core", [(0, 1), (1, 0)])
    own, other = own.reshape(8, BLOCK, D), other.reshape(8, BLOCK, D)

    partner_r = jnp.stack([own[:, PER, :PER], other[:, PER, :PER]]).reshape(1, R).astype(jnp.int32)
    blocks = 2 * jnp.arange(8, dtype=jnp.int32)
    blocks = jnp.stack([blocks + core, blocks + 1 - core]) + row * R_BLOCKS
    ids = (blocks[:, :, None] * PER + jnp.arange(PER, dtype=jnp.int32)).reshape(1, R)

    first = (col * PER).astype(jnp.int32).reshape(1)
    e, z, rsum, csum, pos, cid = scores(first, xc, own, other, ids, partner_r)

    to_rows = by_core(rsum.reshape(2, 8, PER), core).transpose(1, 0, 2).reshape(1, R_BLOCKS, PER)
    sums = jnp.concatenate(
        [
            jnp.broadcast_to(csum[0].reshape(C_BLOCKS, 1, PER), (C_BLOCKS, R_BLOCKS, PER)),
            jnp.broadcast_to(to_rows, (C_BLOCKS, R_BLOCKS, PER)),
            jnp.broadcast_to(jnp.sum(pos), (C_BLOCKS, R_BLOCKS, 128)),
        ],
        axis=2,
    ).reshape(C_BLOCKS * R_BLOCKS, 512)
    sums = lax.all_to_all(sums, ALL, 0, 0, tiled=True).reshape(C_BLOCKS, R_BLOCKS, 512)
    total_r = jnp.sum(sums[:, :, :PER], axis=0)
    total_c = jnp.sum(sums[:, :, PER : 2 * PER], axis=1)
    positives = jnp.sum(sums[:, :, 2 * PER]) * LN2
    ur = by_core((1.0 / total_r).reshape(8, 2, PER).transpose(1, 0, 2), core).reshape(1, R)
    uc = jnp.broadcast_to((1.0 / total_c).reshape(C, 1), (C, 128))
    logs = jnp.sum(jnp.log(total_r)).reshape(1)

    terms = gradients(logs, e, z, ur, uc, partner_r, cid)
    terms = lax.all_to_all(terms.reshape(C_BLOCKS * BLOCK, D), ROW, 0, 0, tiled=True)
    terms = jnp.sum(terms.reshape(C_BLOCKS, BLOCK, D), axis=0)

    mean_objective = (terms[PER, 0] - positives) / VIEWS
    scale = lax.rsqrt(jnp.sum(projections * projections, axis=-1, keepdims=True) + 1e-06)
    z_own = projections * scale
    dz = terms[:PER] / TEMPERATURE
    grad = (dz - z_own * jnp.sum(z_own * dz, axis=-1, keepdims=True)) * scale
    return mean_objective, grad


def solution(mesh):
    fine = Mesh(mesh.devices.reshape(4, 2, 4, 2, 2), ALL)
    placed = (P(ALL, None), P(ALL))
    return jax.shard_map(
        shards, mesh=fine, in_specs=placed, out_specs=(P(), P(ALL, None)), check_vma=False
    )
```

```python
import functools

import jax
import jax.numpy as jnp
from jax import lax
from jax.experimental import pallas as pl
from jax.experimental.pallas import tpu as pltpu
from jax.sharding import Mesh, PartitionSpec as P

f32, bf16 = jnp.float32, jnp.bfloat16
PER = 192
D = 256
VIEWS = 24576
C_BLOCKS = 8
R_BLOCKS = 16
C = C_BLOCKS * PER
R = R_BLOCKS * PER
SPAN = 768
STEPS = R // SPAN
LANES = 256
BLOCK = 200
PAIR = PER + BLOCK
TEMPERATURE = 0.1
LOG2E = 1.4426950408889634
LN2 = 0.6931471805599453
NT = (((1,), (1,)), ((), ()))
ROW = ("y", "zl")
COL = ("x", "zh", "core")
ALL = ROW + COL


def unit(rows):
    return rows * lax.rsqrt(jnp.sum(rows * rows, axis=-1, keepdims=True) + 1e-06)


def halves(a):
    hi = a.astype(bf16)
    return hi, (a - hi.astype(f32)).astype(bf16)


def places():
    y, zl, x, zh, core = (lax.axis_index(a) for a in ALL)
    found = []
    for dz in (0, 1):
        for dy in (0, -1, 1, 2):
            found.append((y + 4 + dy) % 4 * 2 + (zl + dz) % 2)
    for dx in (0, -1, 1, 2):
        for dcore in (0, 1):
            for dz in (0, 1):
                found.append(((x + 4 + dx) % 4 * 2 + (zh + dz) % 2) * 2 + (core + dcore) % 2)
    return found + [(x * 2 + zh) * 2 + core]


def score_kernel(
    c0_ref, c1_ref, c2_ref, c3z_ref, c3a_ref,
    r0_ref, r1_ref, r2_ref, r3z_ref, r3b_ref,
    s0_ref, s1_ref, s2_ref, s3z_ref, s3b_ref,
    e_ref, zr_ref, partner_ref, send_ref,
    a_ref, b_ref, cid_ref, cacc_ref, pacc_ref, rsum_ref, rows_ref,
):
    place = places()
    k = pl.program_id(0)

    @pl.when(k == 0)
    def _():
        cacc_ref[...] = jnp.zeros_like(cacc_ref)
        pacc_ref[...] = jnp.zeros_like(pacc_ref)
        parts = [ref[PER : 2 * PER, :] for ref in (c0_ref, c1_ref, c2_ref)] + [c3z_ref[...]]
        parts += [ref[0:PER, :] for ref in (c0_ref, c1_ref, c2_ref)] + [c3a_ref[...]]
        for s, part in enumerate(parts):
            rows = pl.ds(s * PER, PER)
            hi, lo = halves(unit(part) * (LOG2E / TEMPERATURE))
            a_ref[rows, 0:D] = hi
            a_ref[rows, D : 2 * D] = lo
            a_ref[rows, 2 * D : 3 * D] = hi
            first = (place[s] * R_BLOCKS + place[24]) * PER
            cid_ref[rows, :] = (first + lax.broadcasted_iota(jnp.int32, (PER, 128), 0)).astype(f32)

    def prepare(parts, indices):
        for b in range(4):
            hi, lo = halves(unit(parts[b]))
            rows = pl.ds(b * PER, PER)
            b_ref[rows, 0:D] = hi
            b_ref[rows, D : 2 * D] = hi
            b_ref[rows, 2 * D : 3 * D] = lo
            zr_ref[rows, 0:D] = hi
            zr_ref[rows, D : 2 * D] = lo
            partner_ref[:, b * PER : (b + 1) * PER] = indices[b]

    for step, refs in enumerate(((r0_ref, s0_ref), (r1_ref, s1_ref), (r2_ref, s2_ref))):

        @pl.when(k == step)
        def _():
            parts, indices = [], []
            for ref in refs:
                parts += [ref[BLOCK : BLOCK + PER, :], ref[0:PER, :]]
                indices += [ref[PER : PER + 1, 0:PER], ref[PER + 1 : PER + 2, 0:PER]]
            prepare(parts, indices)

    @pl.when(k == STEPS - 1)
    def _():
        parts, indices = [], []
        for z, b in ((r3z_ref, r3b_ref), (s3z_ref, s3b_ref)):
            parts += [z[BLOCK - PER : BLOCK, :], b[0:PER, :]]
            indices += [z[0:1, 0:PER], b[PER + 1 : PER + 2, 0:PER]]
        prepare(parts, indices)

    cid = cid_ref[...]
    for n in range(SPAN // LANES):
        cols = pl.ds(n * LANES, LANES)
        s = lax.dot_general(a_ref[...], b_ref[cols, :], NT, preferred_element_type=f32)
        row_total = None
        for h in range(LANES // 128):
            lane0 = n * LANES + h * 128
            lanes = pl.ds(lane0, 128)
            part = s[:, h * 128 : (h + 1) * 128]
            e = jnp.exp2(part)
            if lane0 < PER:
                i = lax.broadcasted_iota(jnp.int32, (PER, 128), 0)
                j = lax.broadcasted_iota(jnp.int32, (PER, 128), 1) + lane0
                e = jnp.concatenate([jnp.where((i == j) & (k == 0), 0.0, e[:PER]), e[PER:]])
            hit = jnp.where(cid == partner_ref[:, lanes], part, 0.0)
            e_ref[:, lanes] = e
            rsum_ref[k, 0:1, lanes] = jnp.sum(e, axis=0, keepdims=True)
            pacc_ref[...] += jnp.sum(hit.reshape(C // 8, 8, 128), axis=0)
            row_total = e if row_total is None else row_total + e
        cacc_ref[...] += row_total

    @pl.when(k == STEPS - 1)
    def _():
        csum = lax.dot_general(
            jnp.ones((8, 128), f32), cacc_ref[...], NT, precision=lax.Precision.HIGHEST, preferred_element_type=f32
        )
        positives = jnp.full((R_BLOCKS, 256 - PER), jnp.sum(pacc_ref[...]), f32)
        for s in range(R_BLOCKS):
            step, b = divmod(s, 4)
            rows_ref[place[C_BLOCKS + s], 0:1, 0:PER] = rsum_ref[step, 0:1, b * PER : (b + 1) * PER]
        of_rows = jnp.concatenate([rows_ref[c, 0:1, 0:PER] for c in range(R_BLOCKS)])
        for s in range(C_BLOCKS):
            rows = pl.ds(place[s] * R_BLOCKS, R_BLOCKS)
            mine = jnp.broadcast_to(csum[0:1, s * PER : (s + 1) * PER], (R_BLOCKS, PER))
            send_ref[rows, 0, :] = jnp.concatenate([mine, positives, of_rows, positives], axis=1)


def scores(columns, rows, swapped):
    whole = lambda k: (0, 0)
    arrays = (*columns, *rows, *swapped)
    return pl.pallas_call(
        score_kernel,
        grid=(STEPS,),
        in_specs=[pl.BlockSpec(a.shape, whole) for a in arrays],
        out_specs=[
            pl.BlockSpec((C, SPAN), lambda k: (0, k)),
            pl.BlockSpec((SPAN, 2 * D), lambda k: (k, 0)),
            pl.BlockSpec((1, SPAN), lambda k: (0, k)),
            pl.BlockSpec((C_BLOCKS * R_BLOCKS, 1, 512), lambda k: (0, 0, 0)),
        ],
        out_shape=[
            jax.ShapeDtypeStruct((C, R), f32),
            jax.ShapeDtypeStruct((R, 2 * D), bf16),
            jax.ShapeDtypeStruct((1, R), f32),
            jax.ShapeDtypeStruct((C_BLOCKS * R_BLOCKS, 1, 512), f32),
        ],
        scratch_shapes=[
            pltpu.VMEM((C, 3 * D), bf16),
            pltpu.VMEM((SPAN, 3 * D), bf16),
            pltpu.VMEM((C, 128), f32),
            pltpu.VMEM((C, 128), f32),
            pltpu.VMEM((8, 128), f32),
            pltpu.VMEM((STEPS, 8, SPAN), f32),
            pltpu.VMEM((R_BLOCKS, 8, 256), f32),
        ],
        compiler_params=pltpu.CompilerParams(vmem_limit_bytes=58 << 20),
    )(*arrays)


def gradient_kernel(group, sums_ref, e_ref, z_ref, partner_ref, uc_in_ref, ur_in_ref, *refs):
    first = uc_in_ref is None
    out_refs, refs = refs[:4], refs[4:]
    if first:
        uc_ref, ur_ref, logs_ref, acc_ref, total_ref = refs
    else:
        (acc_ref,) = refs
        uc_ref, ur_ref, logs_ref = uc_in_ref, ur_in_ref, sums_ref
    place = places()
    k = pl.program_id(0)
    half = 4 * PER

    @pl.when(k == 0)
    def _():
        acc_ref[...] = jnp.zeros_like(acc_ref)
        if first:
            total = sums_ref[0:R_BLOCKS, 0, :]
            for r in range(1, C_BLOCKS):
                total = total + sums_ref[r * R_BLOCKS : (r + 1) * R_BLOCKS, 0, :]
            for c in range(R_BLOCKS):
                total_ref[c, 0:1, :] = total[c : c + 1, 0:256]
            logs = jnp.sum(jnp.log(total[:, 0:PER]))
            positives = jnp.sum(total[:, PER : PER + 1]) * LN2
            logs_ref[...] = jnp.full(logs_ref.shape, logs - positives / C_BLOCKS, f32)
            for s in range(R_BLOCKS):
                step, b = divmod(s, 4)
                found = total_ref[place[C_BLOCKS + s], 0:1, 0:PER]
                ur_ref[step, :, b * PER : (b + 1) * PER] = 1.0 / found
            for s in range(C_BLOCKS):
                mine = sums_ref[pl.ds(place[s] * R_BLOCKS, R_BLOCKS), 0, 256 : 256 + PER]
                found = 1.0 / jnp.sum(mine, axis=0, keepdims=True)
                uc_ref[s * PER : (s + 1) * PER, :] = jnp.broadcast_to(found, (128, PER)).T

    uc = uc_ref[group * half : (group + 1) * half, :]
    ids = lax.broadcasted_iota(jnp.int32, (half, 128), 0)
    firsts = [(place[4 * group + i] * R_BLOCKS + place[24]) * PER - i * PER for i in range(4)]
    ids = jnp.concatenate([ids[i * PER : (i + 1) * PER] + firsts[i] for i in range(4)]).astype(f32)
    total = None
    for c in range(0, SPAN, 256):
        his, los = [], []
        for h in range(c, c + 256, 128):
            lanes = pl.ds(h, 128)
            g = e_ref[:, lanes] * (uc + ur_ref[k, :, lanes])
            g = g - jnp.where(ids == partner_ref[:, lanes], 2.0, 0.0)
            hi, lo = halves(g)
            his.append(hi)
            los.append(lo)
        hi, lo = jnp.concatenate(his, axis=1), jnp.concatenate(los, axis=1)
        rows = pl.ds(c, 256)
        both = jnp.dot(jnp.concatenate([hi, lo]), z_ref[rows, 0:D], preferred_element_type=f32)
        rest = jnp.dot(hi, z_ref[rows, D : 2 * D], preferred_element_type=f32)
        part = both[:half] + (both[half:] + rest)
        total = part if total is None else total + part
    acc_ref[...] += total

    @pl.when(k == STEPS - 1)
    def _():
        for i, out_ref in enumerate(out_refs):
            out_ref[0:PER, :] = acc_ref[i * PER : (i + 1) * PER, :]
            out_ref[PER:BLOCK, :] = jnp.broadcast_to(logs_ref[...], (BLOCK - PER, D))


def gradients(group, sums, e, z, partner, weights=None):
    half = 4 * PER
    first = weights is None
    vmem = pl.BlockSpec(memory_space=pltpu.VMEM)
    blocks = [jax.ShapeDtypeStruct((BLOCK, D), f32)] * 4
    if first:
        kernel = lambda s, e, z, i, *refs: gradient_kernel(group, s, e, z, i, None, None, *refs)
        given = ()
        made = [
            jax.ShapeDtypeStruct((C, 128), f32),
            jax.ShapeDtypeStruct((STEPS, 1, SPAN), f32),
            jax.ShapeDtypeStruct((1, D), f32),
        ]
        scratch = [pltpu.VMEM((R_BLOCKS, 8, 256), f32)]
    else:
        kernel = functools.partial(gradient_kernel, group)
        given, made, scratch = weights, [], []
    return pl.pallas_call(
        kernel,
        grid=(STEPS,),
        in_specs=[
            vmem,
            pl.BlockSpec((half, SPAN), lambda k: (group, k)),
            pl.BlockSpec((SPAN, 2 * D), lambda k: (k, 0)),
            pl.BlockSpec((1, SPAN), lambda k: (0, k)),
        ]
        + [vmem] * len(given),
        out_specs=[vmem] * (4 + len(made)),
        out_shape=blocks + made,
        scratch_shapes=[pltpu.VMEM((half, D), f32)] + scratch,
        compiler_params=pltpu.CompilerParams(vmem_limit_bytes=40 << 20),
        cost_estimate=pl.CostEstimate(flops=2 * 3 * half * R * D, bytes_accessed=4 * half * R, transcendentals=0),
    )(sums, e, z, partner, *given)


SWAP = [(0, 1), (1, 0)]
UP = [(i, (i + 1) % 4) for i in range(4)]
DOWN = [(i, (i + 3) % 4) for i in range(4)]


def over_y(terms):
    here, down, up, across = terms
    across = lax.ppermute(across, "y", [(i, (i + 2) % 4) for i in range(4)])
    down = lax.ppermute(down, "y", DOWN)
    up = lax.ppermute(up, "y", UP)
    return here + down + up + across


def shards(projections, partner):
    index = jnp.pad(partner.astype(f32)[None], ((0, 7), (0, D - PER)))
    index, z = lax.optimization_barrier((index, projections))
    index_b = lax.ppermute(index, "zh", SWAP)
    b = lax.ppermute(z, "zh", SWAP)
    a = lax.ppermute(z, "zl", SWAP)
    r0 = jnp.concatenate([b, index[0:1], index_b[0:1], jnp.zeros((6, D), f32), z])
    c0 = jnp.concatenate([a, z])
    c1, c2 = lax.ppermute(c0, "y", UP), lax.ppermute(c0, "y", DOWN)
    r1, r2 = lax.ppermute(r0, "x", UP), lax.ppermute(r0, "x", DOWN)
    c3z, c3a = lax.ppermute(c1[PER:], "y", UP), lax.ppermute(c2[:PER], "y", DOWN)
    r3z, r3b = lax.ppermute(r1[PER:], "x", UP), lax.ppermute(r2[:BLOCK], "x", DOWN)
    s0 = lax.ppermute(r0, "core", SWAP)
    r1, r2, r3z, r3b, c3z, c3a = lax.optimization_barrier((r1, r2, r3z, r3b, c3z, c3a))
    rows = (r0, r1, r2, r3z, r3b)
    swapped = [s0] + [lax.ppermute(r, "core", SWAP) for r in rows[1:]]

    e, zr, partners, sums = scores((c0, c1, c2, c3z, c3a), rows, swapped)
    sums = lax.all_to_all(sums, ALL, 0, 0, tiled=True)
    e, zr, partners = (pltpu.with_memory_space_constraint(v, pltpu.HBM) for v in (e, zr, partners))
    *other, uc, ur, logs = gradients(1, sums, e, zr, partners)
    other = over_y(other)
    same = over_y(gradients(0, logs, e, zr, partners, (uc, ur)))
    terms = same + lax.ppermute(other, "zl", SWAP)

    mean_objective = terms[PER, 0] / VIEWS
    scale = lax.rsqrt(jnp.sum(z * z, axis=-1, keepdims=True) + 1e-06)
    z = z * scale
    dz = terms[:PER] / TEMPERATURE
    grad = (dz - z * jnp.sum(z * dz, axis=-1, keepdims=True)) * scale
    return mean_objective, grad


def solution(mesh):
    fine = Mesh(mesh.devices.reshape(4, 2, 4, 2, 2), ALL)
    placed = (P(ALL, None), P(ALL))
    return jax.shard_map(
        shards, mesh=fine, in_specs=placed, out_specs=(P(), P(ALL, None)), check_vma=False
    )
```

```python
import functools

import jax
import jax.numpy as jnp
from jax import lax
from jax.experimental import pallas as pl
from jax.experimental.pallas import tpu as pltpu
from jax.sharding import Mesh, PartitionSpec as P

f32, bf16 = jnp.float32, jnp.bfloat16
PER = 192
D = 256
VIEWS = 24576
C_BLOCKS = 8
R_BLOCKS = 16
C = C_BLOCKS * PER
R = R_BLOCKS * PER
SPAN = 768
STEPS = R // SPAN
LANES = 256
TILES = SPAN // LANES
BLOCK = 200
PAIR = PER + BLOCK
TEMPERATURE = 0.1
LOG2E = 1.4426950408889634
LN2 = 0.6931471805599453
NT = (((1,), (1,)), ((), ()))
ROW = ("y", "zl")
COL = ("x", "zh", "core")
ALL = ROW + COL


def unit(rows):
    return rows * lax.rsqrt(jnp.sum(rows * rows, axis=-1, keepdims=True) + 1e-06)


def halves(a):
    hi = a.astype(bf16)
    return hi, (a - hi.astype(f32)).astype(bf16)


def places():
    y, zl, x, zh, core = (lax.axis_index(a) for a in ALL)
    found = []
    for dz in (0, 1):
        for dy in (0, -1, 1, 2):
            found.append((y + 4 + dy) % 4 * 2 + (zl + dz) % 2)
    for dx in (0, -1, 1, 2):
        for dcore in (0, 1):
            for dz in (0, 1):
                found.append(((x + 4 + dx) % 4 * 2 + (zh + dz) % 2) * 2 + (core + dcore) % 2)
    return found + [(x * 2 + zh) * 2 + core]


def score_kernel(start, steps, *refs):
    place = places()
    first, last = start == 0, start + steps == STEPS
    if first:
        columns, blocks, refs = refs[:C_BLOCKS], refs[C_BLOCKS : C_BLOCKS + 4], refs[C_BLOCKS + 4 :]
        e_ref, zr_ref, partner_ref, rsum_ref, pos_ref, cacc_ref, a_ref, cid_ref, b_ref = refs
    else:
        blocks, refs = refs[: 4 * steps], refs[4 * steps :]
        a_ref, cid_ref, pos_in_ref, cacc_in_ref = refs[:4]
        refs = refs[7:]
        if last:
            earlier, refs = refs[:start], refs[start:]
            e_ref, zr_ref, partner_ref, send_ref, b_ref, rsum_ref, pos_ref, cacc_ref, rows_ref = refs
        else:
            e_ref, zr_ref, partner_ref, rsum_ref, pos_ref, cacc_ref, b_ref = refs
    j = pl.program_id(0)

    @pl.when(j == 0)
    def _():
        if first:
            cacc_ref[...] = jnp.zeros_like(cacc_ref)
            pos_ref[...] = jnp.zeros_like(pos_ref)
            for s, ref in enumerate(columns):
                rows = pl.ds(s * PER, PER)
                hi, lo = halves(unit(ref[...]) * (LOG2E / TEMPERATURE))
                a_ref[rows, 0:D] = hi
                a_ref[rows, D : 2 * D] = lo
                a_ref[rows, 2 * D : 3 * D] = hi
                start = (place[s] * R_BLOCKS + place[24]) * PER
                cid_ref[rows, :] = (start + lax.broadcasted_iota(jnp.int32, (PER, 128), 0)).astype(f32)
        else:
            cacc_ref[...] = cacc_in_ref[...]
            pos_ref[...] = pos_in_ref[...]

    for step in range(len(blocks) // 4):

        @pl.when(j == step * TILES)
        def _():
            for b, ref in enumerate(blocks[4 * step : 4 * step + 4]):
                hi, lo = halves(unit(ref[0:PER, :]))
                rows = pl.ds(b * PER, PER)
                b_ref[rows, 0:D] = hi
                b_ref[rows, D : 2 * D] = hi
                b_ref[rows, 2 * D : 3 * D] = lo
                zr_ref[rows, 0:D] = hi
                zr_ref[rows, D : 2 * D] = lo
                partner_ref[0, :, b * PER : (b + 1) * PER] = ref[PER : PER + 1, 0:PER]

    cid = cid_ref[...]
    tile = lax.rem(j, TILES) * LANES
    s = lax.dot_general(
        a_ref[...], b_ref[pl.ds(pl.multiple_of(tile, LANES), LANES), :], NT, preferred_element_type=f32
    )
    row_total = None
    for h in range(LANES // 128):
        lanes = pl.ds(pl.multiple_of(tile + h * 128, 128), 128)
        part = s[:, h * 128 : (h + 1) * 128]
        e = jnp.exp2(part)
        if first:
            i = lax.broadcasted_iota(jnp.int32, (PER, 128), 0)
            i2 = lax.broadcasted_iota(jnp.int32, (PER, 128), 1) + h * 128
            e = jnp.concatenate([jnp.where((i == i2) & (j == 0), 0.0, e[:PER]), e[PER:]])
        hit = jnp.where(cid == partner_ref[0, :, lanes], part, 0.0)
        e_ref[0, :, h * 128 : (h + 1) * 128] = e
        rsum_ref[j // TILES, :, lanes] = jnp.sum(e, axis=0, keepdims=True)
        pos_ref[...] += jnp.sum(hit.reshape(C // 8, 8, 128), axis=0)
        row_total = e if row_total is None else row_total + e
    cacc_ref[...] += row_total

    if last:

        @pl.when(j == pl.num_programs(0) - 1)
        def _():
            csum = lax.dot_general(
                jnp.ones((8, 128), f32), cacc_ref[...], NT, precision=lax.Precision.HIGHEST, preferred_element_type=f32
            )
            positives = jnp.full((R_BLOCKS, 256 - PER), jnp.sum(pos_ref[...]), f32)
            for s in range(R_BLOCKS):
                step, b = divmod(s, 4)
                sums = earlier[step][0] if step < start else rsum_ref[step - start]
                rows_ref[place[C_BLOCKS + s], 0:1, 0:PER] = sums[:, b * PER : (b + 1) * PER]
            of_rows = jnp.concatenate([rows_ref[c, 0:1, 0:PER] for c in range(R_BLOCKS)])
            for s in range(C_BLOCKS):
                rows = pl.ds(place[s] * R_BLOCKS, R_BLOCKS)
                mine = jnp.broadcast_to(csum[0:1, s * PER : (s + 1) * PER], (R_BLOCKS, PER))
                send_ref[rows, 0, :] = jnp.concatenate([mine, positives, of_rows, positives], axis=1)


def scores(start, blocks, columns=None, carried=None):
    vmem = pl.BlockSpec(memory_space=pltpu.VMEM)
    steps = len(blocks) // 4
    first, last = start == 0, start + steps == STEPS
    shared = [
        pltpu.HBM((R // LANES, C, LANES), f32),
        pltpu.HBM((R, 2 * D), bf16),
        pltpu.HBM((STEPS, 1, SPAN), f32),
    ]
    shared_specs = [
        pl.BlockSpec((1, C, LANES), lambda j: (start * TILES + j, 0, 0)),
        pl.BlockSpec((SPAN, 2 * D), lambda j: (start + j // TILES, 0)),
        pl.BlockSpec((1, 1, SPAN), lambda j: (start + j // TILES, 0, 0)),
    ]
    sums = [pltpu.VMEM((steps, 1, SPAN), f32), pltpu.VMEM((8, 128), f32), pltpu.VMEM((C, 128), f32)]
    scratch = [pltpu.VMEM((SPAN, 3 * D), bf16)]
    if first:
        given, in_specs, aliases = (*columns, *blocks), [vmem] * (C_BLOCKS + 4), {}
        made = sums + [pltpu.VMEM((C, 3 * D), bf16), pltpu.VMEM((C, 128), f32)]
    else:
        e, zr, partners, rsums, pos, cacc, a, cid = carried
        keep = lambda v: pltpu.with_memory_space_constraint(v, pltpu.VMEM)
        given = (*blocks, *(keep(v) for v in (a, cid, pos, cacc)), e, zr, partners)
        n = len(given) - 3
        in_specs = [vmem] * n + [pl.BlockSpec(memory_space=pl.ANY)] * 3
        aliases = {n: 0, n + 1: 1, n + 2: 2}
        made = sums
        if last:
            given, in_specs = (*given, *(keep(v) for v in rsums)), in_specs + [vmem] * len(rsums)
            made = [jax.ShapeDtypeStruct((C_BLOCKS * R_BLOCKS, 1, 512), f32)]
            scratch += sums + [pltpu.VMEM((R_BLOCKS, 8, 256), f32)]
    size = C * SPAN * steps
    out = pl.pallas_call(
        functools.partial(score_kernel, start, steps),
        grid=(steps * TILES,),
        in_specs=in_specs,
        out_specs=shared_specs + [vmem] * len(made),
        out_shape=shared + made,
        scratch_shapes=scratch,
        input_output_aliases=aliases,
        compiler_params=pltpu.CompilerParams(vmem_limit_bytes=40 << 20),
        cost_estimate=pl.CostEstimate(flops=6 * size * D, bytes_accessed=4 * size, transcendentals=size),
    )(*given)
    if last:
        return out
    e, zr, partners, rsum, pos, cacc = out[:6]
    if first:
        return e, zr, partners, [rsum], pos, cacc, *out[6:]
    return e, zr, partners, [*rsums, rsum], pos, cacc, a, cid


def gradient_kernel(slots, first, sums_ref, *refs):
    count = len(slots)
    e_refs, (z_ref, partner_ref), refs = refs[:count], refs[count : count + 2], refs[count + 2 :]
    if not first:
        (uc_ref, ur_ref), logs_ref, refs = refs[:2], sums_ref, refs[2:]
    out_refs, refs = refs[:count], refs[count:]
    if first:
        uc_ref, ur_ref, logs_ref, acc_ref, total_ref = refs
    else:
        (acc_ref,) = refs
    place = places()
    k = pl.program_id(0)
    rows_here = count * PER

    @pl.when(k == 0)
    def _():
        acc_ref[...] = jnp.zeros_like(acc_ref)
        if first:
            total = sums_ref[0:R_BLOCKS, 0, :]
            for r in range(1, C_BLOCKS):
                total = total + sums_ref[r * R_BLOCKS : (r + 1) * R_BLOCKS, 0, :]
            for c in range(R_BLOCKS):
                total_ref[c, 0:1, :] = total[c : c + 1, 0:256]
            logs = jnp.sum(jnp.log(total[:, 0:PER]))
            positives = jnp.sum(total[:, PER : PER + 1]) * LN2
            logs_ref[...] = jnp.full(logs_ref.shape, logs - positives / C_BLOCKS, f32)
            for s in range(R_BLOCKS):
                step, b = divmod(s, 4)
                found = total_ref[place[C_BLOCKS + s], 0:1, 0:PER]
                ur_ref[step, :, b * PER : (b + 1) * PER] = 1.0 / found
            for s in range(C_BLOCKS):
                mine = sums_ref[pl.ds(place[s] * R_BLOCKS, R_BLOCKS), 0, 256 : 256 + PER]
                found = 1.0 / jnp.sum(mine, axis=0, keepdims=True)
                uc_ref[s * PER : (s + 1) * PER, :] = jnp.broadcast_to(found, (128, PER)).T

    uc = jnp.concatenate([uc_ref[i * PER : (i + 1) * PER, :] for i in slots])
    ids = lax.broadcasted_iota(jnp.int32, (PER, 128), 0)
    ids = jnp.concatenate([ids + (place[i] * R_BLOCKS + place[24]) * PER for i in slots]).astype(f32)
    total = None
    for c in range(0, SPAN, 256):
        his, los = [], []
        for h in range(c, c + 256, 128):
            lanes = pl.ds(h, 128)
            e = jnp.concatenate([e_ref[c // 256, :, h - c : h - c + 128] for e_ref in e_refs])
            g = e * (uc + ur_ref[k, :, lanes])
            g = g - jnp.where(ids == partner_ref[0, :, lanes], 2.0, 0.0)
            hi, lo = halves(g)
            his.append(hi)
            los.append(lo)
        hi, lo = jnp.concatenate(his, axis=1), jnp.concatenate(los, axis=1)
        rows = pl.ds(c, 256)
        both = jnp.dot(jnp.concatenate([hi, lo]), z_ref[rows, 0:D], preferred_element_type=f32)
        rest = jnp.dot(hi, z_ref[rows, D : 2 * D], preferred_element_type=f32)
        part = both[:rows_here] + (both[rows_here:] + rest)
        total = part if total is None else total + part
    acc_ref[...] += total

    @pl.when(k == STEPS - 1)
    def _():
        for i, out_ref in enumerate(out_refs):
            out_ref[0:PER, :] = acc_ref[i * PER : (i + 1) * PER, :]
            out_ref[PER:BLOCK, :] = jnp.broadcast_to(logs_ref[...], (BLOCK - PER, D))


def gradients(slots, sums, e, z, partner, weights=None):
    count = len(slots)
    first = weights is None
    vmem = pl.BlockSpec(memory_space=pltpu.VMEM)
    blocks = [jax.ShapeDtypeStruct((BLOCK, D), f32)] * count
    given, made, scratch = (), [], []
    if first:
        made = [
            jax.ShapeDtypeStruct((C, 128), f32),
            jax.ShapeDtypeStruct((STEPS, 1, SPAN), f32),
            jax.ShapeDtypeStruct((1, D), f32),
        ]
        scratch = [pltpu.VMEM((R_BLOCKS, 8, 256), f32)]
    else:
        given = weights
    size = count * PER * R
    return pl.pallas_call(
        functools.partial(gradient_kernel, slots, first),
        grid=(STEPS,),
        in_specs=[vmem]
        + [pl.BlockSpec((TILES, PER, LANES), lambda k, i=i: (k, i, 0)) for i in slots]
        + [pl.BlockSpec((SPAN, 2 * D), lambda k: (k, 0)), pl.BlockSpec((1, 1, SPAN), lambda k: (k, 0, 0))]
        + [vmem] * len(given),
        out_specs=[vmem] * (count + len(made)),
        out_shape=blocks + made,
        scratch_shapes=[pltpu.VMEM((count * PER, D), f32)] + scratch,
        compiler_params=pltpu.CompilerParams(vmem_limit_bytes=40 << 20),
        cost_estimate=pl.CostEstimate(flops=6 * size * D, bytes_accessed=4 * size, transcendentals=0),
    )(sums, *[e] * count, z, partner, *given)


SWAP = [(0, 1), (1, 0)]
UP = [(i, (i + 1) % 4) for i in range(4)]
DOWN = [(i, (i + 3) % 4) for i in range(4)]


def over_y(down, up, across):
    across = lax.ppermute(across, "y", [(i, (i + 2) % 4) for i in range(4)])
    return lax.ppermute(down, "y", DOWN), lax.ppermute(up, "y", UP), across


def shards(projections, partner):
    index = jnp.pad(partner.astype(f32)[None], ((0, BLOCK - PER - 1), (0, D - PER)))
    z, block = lax.optimization_barrier((projections, jnp.concatenate([projections, index])))
    a = lax.ppermute(z, "zl", SWAP)
    b = lax.ppermute(block, "zh", SWAP)
    c0 = jnp.concatenate([a, z])
    c1, c2 = lax.ppermute(c0, "y", UP), lax.ppermute(c0, "y", DOWN)
    c3z, c3a = lax.ppermute(c1[PER:], "y", UP), lax.ppermute(c2[:PER], "y", DOWN)
    r0 = jnp.concatenate([b, block])
    r1, r2 = lax.ppermute(r0, "x", UP), lax.ppermute(r0, "x", DOWN)
    r3z, r3b = lax.ppermute(r1[BLOCK:], "x", UP), lax.ppermute(r2[:BLOCK], "x", DOWN)
    swap = lambda r: lax.ppermute(r, "core", SWAP)
    columns = (z, c1[PER:], c2[PER:], c3z, a, c1[:PER], c2[:PER], c3a)
    rows = [(r[BLOCK:], r[:BLOCK], q[BLOCK:], q[:BLOCK]) for r, q in ((r, swap(r)) for r in (r0, r1, r2))]
    carried = scores(0, rows[0], columns)
    carried = scores(1, rows[1], carried=carried)
    e, zr, partners, sums = scores(2, (*rows[2], r3z, r3b, swap(r3z), swap(r3b)), carried=carried)
    sums = lax.all_to_all(sums, ALL, 0, 0, tiled=True)
    e, zr, partners = (pltpu.with_memory_space_constraint(v, pltpu.HBM) for v in (e, zr, partners))
    here, *away, uc, ur, logs = gradients((4, 5, 6, 7), sums, e, zr, partners)
    other = sum(over_y(*away), here)
    away = gradients((1, 2, 3), logs, e, zr, partners, (uc, ur))
    logs, other = lax.optimization_barrier((logs, other))
    (here,) = gradients((0,), logs, e, zr, partners, (uc, ur))
    terms = sum(over_y(*away), here) + lax.ppermute(other, "zl", SWAP)
    z, _ = lax.optimization_barrier((z, other))

    mean_objective = terms[PER, 0] / VIEWS
    scale = lax.rsqrt(jnp.sum(z * z, axis=-1, keepdims=True) + 1e-06)
    z = z * scale
    dz = terms[:PER] / TEMPERATURE
    grad = (dz - z * jnp.sum(z * dz, axis=-1, keepdims=True)) * scale
    return mean_objective, grad


def solution(mesh):
    fine = Mesh(mesh.devices.reshape(4, 2, 4, 2, 2), ALL)
    placed = (P(ALL, None), P(ALL))
    return jax.shard_map(
        shards, mesh=fine, in_specs=placed, out_specs=(P(), P(ALL, None)), check_vma=False
    )
```

```python
import functools

import jax
import jax.numpy as jnp
from jax import lax
from jax.experimental import pallas as pl
from jax.experimental.pallas import tpu as pltpu
from jax.sharding import Mesh, PartitionSpec as P

f32, bf16 = jnp.float32, jnp.bfloat16
PER = 192
D = 256
VIEWS = 24576
C_BLOCKS = 8
R_BLOCKS = 16
C = C_BLOCKS * PER
R = R_BLOCKS * PER
SPAN = 768
STEPS = R // SPAN
LANES = 256
TILES = SPAN // LANES
WIDE = 2
BLOCK = 200
PAIR = PER + BLOCK
TEMPERATURE = 0.1
LOG2E = 1.4426950408889634
LN2 = 0.6931471805599453
NT = (((1,), (1,)), ((), ()))
ROW = ("y", "zl")
COL = ("x", "zh", "core")
ALL = ROW + COL


def unit(rows):
    return rows * lax.rsqrt(jnp.sum(rows * rows, axis=-1, keepdims=True) + 1e-06)


def halves(a):
    hi = a.astype(bf16)
    return hi, (a - hi.astype(f32)).astype(bf16)


def places():
    y, zl, x, zh, core = (lax.axis_index(a) for a in ALL)
    found = []
    for dz in (0, 1):
        for dy in (0, -1, 1, 2):
            found.append((y + 4 + dy) % 4 * 2 + (zl + dz) % 2)
    for dx in (0, -1, 1, 2):
        for dcore in (0, 1):
            for dz in (0, 1):
                found.append(((x + 4 + dx) % 4 * 2 + (zh + dz) % 2) * 2 + (core + dcore) % 2)
    return found + [(x * 2 + zh) * 2 + core]


def score_kernel(start, steps, *refs):
    place = places()
    first, last = start == 0, start + steps == STEPS
    if first:
        columns, blocks, refs = refs[:C_BLOCKS], refs[C_BLOCKS : C_BLOCKS + 4], refs[C_BLOCKS + 4 :]
        e_ref, zr_ref, partner_ref, rsum_ref, pos_ref, cacc_ref, a_ref, cid_ref, b_ref = refs
    else:
        blocks, refs = refs[: 4 * steps], refs[4 * steps :]
        a_ref, cid_ref, pos_in_ref, cacc_in_ref = refs[:4]
        refs = refs[7:]
        if last:
            earlier, refs = refs[:start], refs[start:]
            e_ref, zr_ref, partner_ref, send_ref, b_ref, rsum_ref, pos_ref, cacc_ref, rows_ref = refs
        else:
            e_ref, zr_ref, partner_ref, rsum_ref, pos_ref, cacc_ref, b_ref = refs
    j = pl.program_id(0)

    @pl.when(j == 0)
    def _():
        if first:
            cacc_ref[...] = jnp.zeros_like(cacc_ref)
            pos_ref[...] = jnp.zeros_like(pos_ref)
            for s, ref in enumerate(columns):
                rows = pl.ds(s * PER, PER)
                hi, lo = halves(unit(ref[...]) * (LOG2E / TEMPERATURE))
                a_ref[rows, 0:D] = hi
                a_ref[rows, D : 2 * D] = lo
                a_ref[rows, 2 * D : 3 * D] = hi
                start = (place[s] * R_BLOCKS + place[24]) * PER
                cid_ref[rows, :] = (start + lax.broadcasted_iota(jnp.int32, (PER, 128), 0)).astype(f32)
        else:
            cacc_ref[...] = cacc_in_ref[...]
            pos_ref[...] = pos_in_ref[...]

    for step in range(len(blocks) // 4):

        @pl.when(j == step * TILES)
        def _():
            for b, ref in enumerate(blocks[4 * step : 4 * step + 4]):
                hi, lo = halves(unit(ref[0:PER, :]))
                rows = pl.ds(b * PER, PER)
                b_ref[rows, 0:D] = hi
                b_ref[rows, D : 2 * D] = hi
                b_ref[rows, 2 * D : 3 * D] = lo
                zr_ref[rows, 0:D] = hi
                zr_ref[rows, D : 2 * D] = lo
                partner_ref[0, :, b * PER : (b + 1) * PER] = ref[PER : PER + 1, 0:PER]

    cid = cid_ref[...]
    tile = lax.rem(j, TILES) * LANES
    s = lax.dot_general(
        a_ref[...], b_ref[pl.ds(pl.multiple_of(tile, LANES), LANES), :], NT, preferred_element_type=f32
    )
    row_total = None
    for h in range(LANES // 128):
        lanes = pl.ds(pl.multiple_of(tile + h * 128, 128), 128)
        part = s[:, h * 128 : (h + 1) * 128]
        e = jnp.exp2(part)
        if first:
            i = lax.broadcasted_iota(jnp.int32, (PER, 128), 0)
            i2 = lax.broadcasted_iota(jnp.int32, (PER, 128), 1) + h * 128
            e = jnp.concatenate([jnp.where((i == i2) & (j == 0), 0.0, e[:PER]), e[PER:]])
        hit = jnp.where(cid == partner_ref[0, :, lanes], part, 0.0)
        e_ref[0, :, h * 128 : (h + 1) * 128] = e
        rsum_ref[j // TILES, :, lanes] = jnp.sum(e, axis=0, keepdims=True)
        pos_ref[...] += jnp.sum(hit.reshape(C // 8, 8, 128), axis=0)
        row_total = e if row_total is None else row_total + e
    cacc_ref[...] += row_total

    if last:

        @pl.when(j == pl.num_programs(0) - 1)
        def _():
            csum = lax.dot_general(
                jnp.ones((8, 128), f32), cacc_ref[...], NT, precision=lax.Precision.HIGHEST, preferred_element_type=f32
            )
            positives = jnp.full((R_BLOCKS, 256 - PER), jnp.sum(pos_ref[...]), f32)
            for s in range(R_BLOCKS):
                step, b = divmod(s, 4)
                sums = earlier[step][0] if step < start else rsum_ref[step - start]
                rows_ref[place[C_BLOCKS + s], 0:1, 0:PER] = sums[:, b * PER : (b + 1) * PER]
            of_rows = jnp.concatenate([rows_ref[c, 0:1, 0:PER] for c in range(R_BLOCKS)])
            for s in range(C_BLOCKS):
                rows = pl.ds(place[s] * R_BLOCKS, R_BLOCKS)
                mine = jnp.broadcast_to(csum[0:1, s * PER : (s + 1) * PER], (R_BLOCKS, PER))
                send_ref[rows, 0, :] = jnp.concatenate([mine, positives, of_rows, positives], axis=1)


def scores(start, blocks, columns=None, carried=None):
    vmem = pl.BlockSpec(memory_space=pltpu.VMEM)
    steps = len(blocks) // 4
    first, last = start == 0, start + steps == STEPS
    shared = [
        pltpu.HBM((R // LANES, C, LANES), f32),
        pltpu.HBM((R, 2 * D), bf16),
        pltpu.HBM((STEPS, 1, SPAN), f32),
    ]
    shared_specs = [
        pl.BlockSpec((1, C, LANES), lambda j: (start * TILES + j, 0, 0)),
        pl.BlockSpec((SPAN, 2 * D), lambda j: (start + j // TILES, 0)),
        pl.BlockSpec((1, 1, SPAN), lambda j: (start + j // TILES, 0, 0)),
    ]
    sums = [pltpu.VMEM((steps, 1, SPAN), f32), pltpu.VMEM((8, 128), f32), pltpu.VMEM((C, 128), f32)]
    scratch = [pltpu.VMEM((SPAN, 3 * D), bf16)]
    if first:
        given, in_specs, aliases = (*columns, *blocks), [vmem] * (C_BLOCKS + 4), {}
        made = sums + [pltpu.VMEM((C, 3 * D), bf16), pltpu.VMEM((C, 128), f32)]
    else:
        e, zr, partners, rsums, pos, cacc, a, cid = carried
        keep = lambda v: pltpu.with_memory_space_constraint(v, pltpu.VMEM)
        given = (*blocks, *(keep(v) for v in (a, cid, pos, cacc)), e, zr, partners)
        n = len(given) - 3
        in_specs = [vmem] * n + [pl.BlockSpec(memory_space=pl.ANY)] * 3
        aliases = {n: 0, n + 1: 1, n + 2: 2}
        made = sums
        if last:
            given, in_specs = (*given, *(keep(v) for v in rsums)), in_specs + [vmem] * len(rsums)
            made = [jax.ShapeDtypeStruct((C_BLOCKS * R_BLOCKS, 1, 512), f32)]
            scratch += sums + [pltpu.VMEM((R_BLOCKS, 8, 256), f32)]
    size = C * SPAN * steps
    out = pl.pallas_call(
        functools.partial(score_kernel, start, steps),
        grid=(steps * TILES,),
        in_specs=in_specs,
        out_specs=shared_specs + [vmem] * len(made),
        out_shape=shared + made,
        scratch_shapes=scratch,
        input_output_aliases=aliases,
        compiler_params=pltpu.CompilerParams(vmem_limit_bytes=40 << 20),
        cost_estimate=pl.CostEstimate(flops=6 * size * D, bytes_accessed=4 * size, transcendentals=size),
    )(*given)
    if last:
        return out
    e, zr, partners, rsum, pos, cacc = out[:6]
    if first:
        return e, zr, partners, [rsum], pos, cacc, *out[6:]
    return e, zr, partners, [*rsums, rsum], pos, cacc, a, cid


def gradient_kernel(slots, first, sums_ref, *refs):
    count = len(slots)
    e_refs, (z_ref, partner_ref), refs = refs[:count], refs[count : count + 2], refs[count + 2 :]
    if not first:
        (uc_ref, ur_ref), logs_ref, refs = refs[:2], sums_ref, refs[2:]
    out_refs, refs = refs[:count], refs[count:]
    if first:
        uc_ref, ur_ref, logs_ref, acc_ref, total_ref = refs
    else:
        (acc_ref,) = refs
    place = places()
    k = pl.program_id(0)
    rows_here = count * PER

    @pl.when(k == 0)
    def _():
        acc_ref[...] = jnp.zeros_like(acc_ref)
        if first:
            total = sums_ref[0:R_BLOCKS, 0, :]
            for r in range(1, C_BLOCKS):
                total = total + sums_ref[r * R_BLOCKS : (r + 1) * R_BLOCKS, 0, :]
            for c in range(R_BLOCKS):
                total_ref[c, 0:1, :] = total[c : c + 1, 0:256]
            logs = jnp.sum(jnp.log(total[:, 0:PER]))
            positives = jnp.sum(total[:, PER : PER + 1]) * LN2
            logs_ref[...] = jnp.full(logs_ref.shape, logs - positives / C_BLOCKS, f32)
            for s in range(R_BLOCKS):
                step, b = divmod(s, 4)
                found = total_ref[place[C_BLOCKS + s], 0:1, 0:PER]
                ur_ref[step, :, b * PER : (b + 1) * PER] = 1.0 / found
            for s in range(C_BLOCKS):
                mine = sums_ref[pl.ds(place[s] * R_BLOCKS, R_BLOCKS), 0, 256 : 256 + PER]
                found = 1.0 / jnp.sum(mine, axis=0, keepdims=True)
                uc_ref[s * PER : (s + 1) * PER, :] = jnp.broadcast_to(found, (128, PER)).T

    uc = jnp.concatenate([uc_ref[i * PER : (i + 1) * PER, :] for i in slots])
    ids = lax.broadcasted_iota(jnp.int32, (PER, 128), 0)
    ids = jnp.concatenate([ids + (place[i] * R_BLOCKS + place[24]) * PER for i in slots]).astype(f32)
    total = None
    for c in range(0, WIDE * SPAN, 256):
        his, los = [], []
        for h in range(c, c + 256, 128):
            part, lanes = h // SPAN, pl.ds(h % SPAN, 128)
            e = jnp.concatenate([e_ref[c // 256, :, h - c : h - c + 128] for e_ref in e_refs])
            g = e * (uc + ur_ref[WIDE * k + part, :, lanes])
            g = g - jnp.where(ids == partner_ref[part, :, lanes], 2.0, 0.0)
            hi, lo = halves(g)
            his.append(hi)
            los.append(lo)
        hi, lo = jnp.concatenate(his, axis=1), jnp.concatenate(los, axis=1)
        rows = pl.ds(c, 256)
        both = jnp.dot(jnp.concatenate([hi, lo]), z_ref[rows, 0:D], preferred_element_type=f32)
        rest = jnp.dot(hi, z_ref[rows, D : 2 * D], preferred_element_type=f32)
        part = both[:rows_here] + (both[rows_here:] + rest)
        total = part if total is None else total + part
    acc_ref[...] += total

    @pl.when(k == STEPS // WIDE - 1)
    def _():
        for i, out_ref in enumerate(out_refs):
            out_ref[0:PER, :] = acc_ref[i * PER : (i + 1) * PER, :]
            out_ref[PER:BLOCK, :] = jnp.broadcast_to(logs_ref[...], (BLOCK - PER, D))


def gradients(slots, sums, e, z, partner, weights=None):
    count = len(slots)
    first = weights is None
    vmem = pl.BlockSpec(memory_space=pltpu.VMEM)
    blocks = [jax.ShapeDtypeStruct((BLOCK, D), f32)] * count
    given, made, scratch = (), [], []
    if first:
        made = [
            jax.ShapeDtypeStruct((C, 128), f32),
            jax.ShapeDtypeStruct((STEPS, 1, SPAN), f32),
            jax.ShapeDtypeStruct((1, D), f32),
        ]
        scratch = [pltpu.VMEM((R_BLOCKS, 8, 256), f32)]
    else:
        given = weights
    size = count * PER * R
    return pl.pallas_call(
        functools.partial(gradient_kernel, slots, first),
        grid=(STEPS // WIDE,),
        in_specs=[vmem]
        + [pl.BlockSpec((WIDE * TILES, PER, LANES), lambda k, i=i: (k, i, 0)) for i in slots]
        + [pl.BlockSpec((WIDE * SPAN, 2 * D), lambda k: (k, 0)), pl.BlockSpec((WIDE, 1, SPAN), lambda k: (k, 0, 0))]
        + [vmem] * len(given),
        out_specs=[vmem] * (count + len(made)),
        out_shape=blocks + made,
        scratch_shapes=[pltpu.VMEM((count * PER, D), f32)] + scratch,
        compiler_params=pltpu.CompilerParams(vmem_limit_bytes=40 << 20),
        cost_estimate=pl.CostEstimate(flops=6 * size * D, bytes_accessed=4 * size, transcendentals=0),
    )(sums, *[e] * count, z, partner, *given)


def finish_kernel(z_ref, *refs):
    *term_refs, mean_ref, grad_ref = refs
    total = term_refs[0][...]
    for ref in term_refs[1:]:
        total = total + ref[...]
    mean_ref[0, 0] = jnp.sum(total[PER : PER + 1, 0:1]) / VIEWS
    z = z_ref[...]
    scale = lax.rsqrt(jnp.sum(z * z, axis=-1, keepdims=True) + 1e-06)
    z = z * scale
    dz = total[0:PER, :] * (1.0 / TEMPERATURE)
    grad_ref[...] = (dz - z * jnp.sum(z * dz, axis=-1, keepdims=True)) * scale


def finish(z, *terms):
    return pl.pallas_call(
        finish_kernel,
        in_specs=[pl.BlockSpec(memory_space=pltpu.VMEM)] * (1 + len(terms)),
        out_specs=[pl.BlockSpec(memory_space=pltpu.SMEM), pl.BlockSpec(memory_space=pltpu.VMEM)],
        out_shape=[jax.ShapeDtypeStruct((1, 1), f32), jax.ShapeDtypeStruct((PER, D), f32)],
        compiler_params=pltpu.CompilerParams(vmem_limit_bytes=16 << 20),
    )(z, *terms)


def pack_kernel(z_ref, partner_ref, out_ref):
    out_ref[0:PER, :] = z_ref[...]
    out_ref[PER:BLOCK, :] = jnp.zeros((BLOCK - PER, D), f32)
    out_ref[PER : PER + 1, 0:PER] = partner_ref[...].reshape(1, PER).astype(f32)


def pack(z, partner):
    return pl.pallas_call(
        pack_kernel,
        in_specs=[pl.BlockSpec(memory_space=pltpu.VMEM)] * 2,
        out_specs=pl.BlockSpec(memory_space=pltpu.VMEM),
        out_shape=jax.ShapeDtypeStruct((BLOCK, D), f32),
        compiler_params=pltpu.CompilerParams(vmem_limit_bytes=16 << 20),
    )(z, partner)


SWAP = [(0, 1), (1, 0)]
UP = [(i, (i + 1) % 4) for i in range(4)]
DOWN = [(i, (i + 3) % 4) for i in range(4)]


def over_y(down, up, across):
    across = lax.ppermute(across, "y", [(i, (i + 2) % 4) for i in range(4)])
    return lax.ppermute(down, "y", DOWN), lax.ppermute(up, "y", UP), across


def shards(projections, partner):
    here = (pltpu.with_memory_space_constraint(v, pltpu.HBM) for v in (projections, partner))
    z, block = lax.optimization_barrier((projections, pack(*here)))
    a = lax.ppermute(z, "zl", SWAP)
    b = lax.ppermute(block, "zh", SWAP)
    c0 = jnp.concatenate([a, z])
    c1, c2 = lax.ppermute(c0, "y", UP), lax.ppermute(c0, "y", DOWN)
    c3z, c3a = lax.ppermute(c1[PER:], "y", UP), lax.ppermute(c2[:PER], "y", DOWN)
    r0 = jnp.concatenate([b, block])
    r1, r2 = lax.ppermute(r0, "x", UP), lax.ppermute(r0, "x", DOWN)
    r3z, r3b = lax.ppermute(r1[BLOCK:], "x", UP), lax.ppermute(r2[:BLOCK], "x", DOWN)
    swap = lambda r: lax.ppermute(r, "core", SWAP)
    columns = (z, c1[PER:], c2[PER:], c3z, a, c1[:PER], c2[:PER], c3a)
    rows = [(r[BLOCK:], r[:BLOCK], q[BLOCK:], q[:BLOCK]) for r, q in ((r, swap(r)) for r in (r0, r1, r2))]
    carried = scores(0, rows[0], columns)
    carried = scores(1, rows[1], carried=carried)
    e, zr, partners, sums = scores(2, (*rows[2], r3z, r3b, swap(r3z), swap(r3b)), carried=carried)
    sums = lax.all_to_all(sums, ALL, 0, 0, tiled=True)
    e, zr, partners = (pltpu.with_memory_space_constraint(v, pltpu.HBM) for v in (e, zr, partners))
    here, *away, uc, ur, logs = gradients((4, 5, 6, 7), sums, e, zr, partners)
    other = sum(over_y(*away), here)
    away = gradients((1, 2, 3), logs, e, zr, partners, (uc, ur))
    logs, other = lax.optimization_barrier((logs, other))
    (here,) = gradients((0,), logs, e, zr, partners, (uc, ur))
    mean_objective, grad = finish(z, here, *over_y(*away), lax.ppermute(other, "zl", SWAP))
    return mean_objective[0, 0], grad


def solution(mesh):
    fine = Mesh(mesh.devices.reshape(4, 2, 4, 2, 2), ALL)
    placed = (P(ALL, None), P(ALL))
    return jax.shard_map(
        shards, mesh=fine, in_specs=placed, out_specs=(P(), P(ALL, None)), check_vma=False
    )
```

```python
import functools

import jax
import jax.numpy as jnp
from jax import lax
from jax.experimental import pallas as pl
from jax.experimental.pallas import tpu as pltpu
from jax.sharding import Mesh, PartitionSpec as P

f32, bf16 = jnp.float32, jnp.bfloat16
PER = 192
D = 256
VIEWS = 24576
C_BLOCKS = 8
R_BLOCKS = 16
C = C_BLOCKS * PER
R = R_BLOCKS * PER
SPAN = 768
STEPS = R // SPAN
LANES = 256
TILES = SPAN // LANES
WIDE = 2
BLOCK = 200
PAIR = PER + BLOCK
TEMPERATURE = 0.1
LOG2E = 1.4426950408889634
LN2 = 0.6931471805599453
NT = (((1,), (1,)), ((), ()))
ROW = ("y", "zl")
COL = ("x", "zh", "core")
ALL = ROW + COL


def unit(rows):
    return rows * lax.rsqrt(jnp.sum(rows * rows, axis=-1, keepdims=True) + 1e-06)


def halves(a):
    hi = a.astype(bf16)
    return hi, (a - hi.astype(f32)).astype(bf16)


def places():
    y, zl, x, zh, core = (lax.axis_index(a) for a in ALL)
    found = []
    for dz in (0, 1):
        for dy in (0, -1, 1, 2):
            found.append((y + 4 + dy) % 4 * 2 + (zl + dz) % 2)
    for dx in (0, -1, 1, 2):
        for dcore in (0, 1):
            for dz in (0, 1):
                found.append(((x + 4 + dx) % 4 * 2 + (zh + dz) % 2) * 2 + (core + dcore) % 2)
    return found + [(x * 2 + zh) * 2 + core]


def score_kernel(start, steps, *refs):
    place = places()
    first, last = start == 0, start + steps == STEPS
    if first:
        columns, blocks, refs = refs[:C_BLOCKS], refs[C_BLOCKS : C_BLOCKS + 4], refs[C_BLOCKS + 4 :]
        e_ref, zr_ref, partner_ref, rsum_ref, pos_ref, cacc_ref, a_ref, cid_ref, b_ref = refs
    else:
        blocks, refs = refs[: 4 * steps], refs[4 * steps :]
        a_ref, cid_ref, pos_in_ref, cacc_in_ref = refs[:4]
        refs = refs[7:]
        if last:
            earlier, refs = refs[:start], refs[start:]
            e_ref, zr_ref, partner_ref, send_ref, b_ref, rsum_ref, pos_ref, cacc_ref, rows_ref = refs
        else:
            e_ref, zr_ref, partner_ref, rsum_ref, pos_ref, cacc_ref, b_ref = refs
    j = pl.program_id(0)

    @pl.when(j == 0)
    def _():
        if first:
            cacc_ref[...] = jnp.zeros_like(cacc_ref)
            pos_ref[...] = jnp.zeros_like(pos_ref)
            for s, ref in enumerate(columns):
                rows = pl.ds(s * PER, PER)
                hi, lo = halves(unit(ref[...]) * (LOG2E / TEMPERATURE))
                a_ref[rows, 0:D] = hi
                a_ref[rows, D : 2 * D] = lo
                a_ref[rows, 2 * D : 3 * D] = hi
                start = (place[s] * R_BLOCKS + place[24]) * PER
                cid_ref[rows, :] = (start + lax.broadcasted_iota(jnp.int32, (PER, 128), 0)).astype(f32)
        else:
            cacc_ref[...] = cacc_in_ref[...]
            pos_ref[...] = pos_in_ref[...]

    for step in range(len(blocks) // 4):

        @pl.when(j == step * TILES)
        def _():
            for b, ref in enumerate(blocks[4 * step : 4 * step + 4]):
                hi, lo = halves(unit(ref[0:PER, :]))
                rows = pl.ds(b * PER, PER)
                b_ref[rows, 0:D] = hi
                b_ref[rows, D : 2 * D] = hi
                b_ref[rows, 2 * D : 3 * D] = lo
                zr_ref[rows, 0:D] = hi
                zr_ref[rows, D : 2 * D] = lo
                partner_ref[0, :, b * PER : (b + 1) * PER] = ref[PER : PER + 1, 0:PER]

    cid = cid_ref[...]
    tile = lax.rem(j, TILES) * LANES
    s = lax.dot_general(
        a_ref[...], b_ref[pl.ds(pl.multiple_of(tile, LANES), LANES), :], NT, preferred_element_type=f32
    )
    row_total = None
    for h in range(LANES // 128):
        lanes = pl.ds(pl.multiple_of(tile + h * 128, 128), 128)
        part = s[:, h * 128 : (h + 1) * 128]
        e = jnp.exp2(part)
        if first:
            i = lax.broadcasted_iota(jnp.int32, (PER, 128), 0)
            i2 = lax.broadcasted_iota(jnp.int32, (PER, 128), 1) + h * 128
            e = jnp.concatenate([jnp.where((i == i2) & (j == 0), 0.0, e[:PER]), e[PER:]])
        hit = jnp.where(cid == partner_ref[0, :, lanes], part, 0.0)
        e_ref[0, :, h * 128 : (h + 1) * 128] = e
        rsum_ref[j // TILES, :, lanes] = jnp.sum(e, axis=0, keepdims=True)
        pos_ref[...] += jnp.sum(hit.reshape(C // 8, 8, 128), axis=0)
        row_total = e if row_total is None else row_total + e
    cacc_ref[...] += row_total

    if last:

        @pl.when(j == pl.num_programs(0) - 1)
        def _():
            csum = lax.dot_general(
                jnp.ones((8, 128), f32), cacc_ref[...], NT, precision=lax.Precision.HIGHEST, preferred_element_type=f32
            )
            positives = jnp.full((R_BLOCKS, 256 - PER), jnp.sum(pos_ref[...]), f32)
            for s in range(R_BLOCKS):
                step, b = divmod(s, 4)
                sums = earlier[step][0] if step < start else rsum_ref[step - start]
                rows_ref[place[C_BLOCKS + s], 0:1, 0:PER] = sums[:, b * PER : (b + 1) * PER]
            of_rows = jnp.concatenate([rows_ref[c, 0:1, 0:PER] for c in range(R_BLOCKS)])
            for s in range(C_BLOCKS):
                rows = pl.ds(place[s] * R_BLOCKS, R_BLOCKS)
                mine = jnp.broadcast_to(csum[0:1, s * PER : (s + 1) * PER], (R_BLOCKS, PER))
                send_ref[rows, 0, :] = jnp.concatenate([mine, positives, of_rows, positives], axis=1)


def scores(start, blocks, columns=None, carried=None):
    vmem = pl.BlockSpec(memory_space=pltpu.VMEM)
    steps = len(blocks) // 4
    first, last = start == 0, start + steps == STEPS
    shared = [
        pltpu.HBM((R // LANES, C, LANES), f32),
        pltpu.HBM((R, 2 * D), bf16),
        pltpu.HBM((STEPS, 1, SPAN), f32),
    ]
    shared_specs = [
        pl.BlockSpec((1, C, LANES), lambda j: (start * TILES + j, 0, 0)),
        pl.BlockSpec((SPAN, 2 * D), lambda j: (start + j // TILES, 0)),
        pl.BlockSpec((1, 1, SPAN), lambda j: (start + j // TILES, 0, 0)),
    ]
    sums = [pltpu.VMEM((steps, 1, SPAN), f32), pltpu.VMEM((8, 128), f32), pltpu.VMEM((C, 128), f32)]
    scratch = [pltpu.VMEM((SPAN, 3 * D), bf16)]
    if first:
        given, in_specs, aliases = (*columns, *blocks), [vmem] * (C_BLOCKS + 4), {}
        made = sums + [pltpu.VMEM((C, 3 * D), bf16), pltpu.VMEM((C, 128), f32)]
    else:
        e, zr, partners, rsums, pos, cacc, a, cid = carried
        keep = lambda v: pltpu.with_memory_space_constraint(v, pltpu.VMEM)
        given = (*blocks, *(keep(v) for v in (a, cid, pos, cacc)), e, zr, partners)
        n = len(given) - 3
        in_specs = [vmem] * n + [pl.BlockSpec(memory_space=pl.ANY)] * 3
        aliases = {n: 0, n + 1: 1, n + 2: 2}
        made = sums
        if last:
            given, in_specs = (*given, *(keep(v) for v in rsums)), in_specs + [vmem] * len(rsums)
            made = [jax.ShapeDtypeStruct((C_BLOCKS * R_BLOCKS, 1, 512), f32)]
            scratch += sums + [pltpu.VMEM((R_BLOCKS, 8, 256), f32)]
    size = C * SPAN * steps
    out = pl.pallas_call(
        functools.partial(score_kernel, start, steps),
        grid=(steps * TILES,),
        in_specs=in_specs,
        out_specs=shared_specs + [vmem] * len(made),
        out_shape=shared + made,
        scratch_shapes=scratch,
        input_output_aliases=aliases,
        compiler_params=pltpu.CompilerParams(vmem_limit_bytes=40 << 20),
        cost_estimate=pl.CostEstimate(flops=6 * size * D, bytes_accessed=4 * size, transcendentals=size),
    )(*given)
    if last:
        return out
    e, zr, partners, rsum, pos, cacc = out[:6]
    if first:
        return e, zr, partners, [rsum], pos, cacc, *out[6:]
    return e, zr, partners, [*rsums, rsum], pos, cacc, a, cid


def gradient_kernel(slots, first, sums_ref, *refs):
    count = len(slots)
    e_refs, (z_ref, partner_ref), refs = refs[:count], refs[count : count + 2], refs[count + 2 :]
    if not first:
        (uc_ref, ur_ref), logs_ref, refs = refs[:2], sums_ref, refs[2:]
    out_refs, refs = refs[:count], refs[count:]
    if first:
        uc_ref, ur_ref, logs_ref, acc_ref, total_ref = refs
    else:
        (acc_ref,) = refs
    place = places()
    k = pl.program_id(0)
    rows_here = count * PER

    @pl.when(k == 0)
    def _():
        acc_ref[...] = jnp.zeros_like(acc_ref)
        if first:
            total = sums_ref[0:R_BLOCKS, 0, :]
            for r in range(1, C_BLOCKS):
                total = total + sums_ref[r * R_BLOCKS : (r + 1) * R_BLOCKS, 0, :]
            for c in range(R_BLOCKS):
                total_ref[c, 0:1, :] = total[c : c + 1, 0:256]
            logs = jnp.sum(jnp.log(total[:, 0:PER]))
            positives = jnp.sum(total[:, PER : PER + 1]) * LN2
            logs_ref[...] = jnp.full(logs_ref.shape, logs - positives / C_BLOCKS, f32)
            for s in range(R_BLOCKS):
                step, b = divmod(s, 4)
                found = total_ref[place[C_BLOCKS + s], 0:1, 0:PER]
                ur_ref[step, :, b * PER : (b + 1) * PER] = 1.0 / found
            for s in range(C_BLOCKS):
                mine = sums_ref[pl.ds(place[s] * R_BLOCKS, R_BLOCKS), 0, 256 : 256 + PER]
                found = 1.0 / jnp.sum(mine, axis=0, keepdims=True)
                uc_ref[s * PER : (s + 1) * PER, :] = jnp.broadcast_to(found, (128, PER)).T

    uc = jnp.concatenate([uc_ref[i * PER : (i + 1) * PER, :] for i in slots])
    ids = lax.broadcasted_iota(jnp.int32, (PER, 128), 0)
    ids = jnp.concatenate([ids + (place[i] * R_BLOCKS + place[24]) * PER for i in slots]).astype(f32)
    total = None
    for c in range(0, WIDE * SPAN, 256):
        his, los = [], []
        for h in range(c, c + 256, 128):
            part, lanes = h // SPAN, pl.ds(h % SPAN, 128)
            e = jnp.concatenate([e_ref[c // 256, :, h - c : h - c + 128] for e_ref in e_refs])
            g = e * (uc + ur_ref[WIDE * k + part, :, lanes])
            g = g - jnp.where(ids == partner_ref[part, :, lanes], 2.0, 0.0)
            hi, lo = halves(g)
            his.append(hi)
            los.append(lo)
        hi, lo = jnp.concatenate(his, axis=1), jnp.concatenate(los, axis=1)
        rows = pl.ds(c, 256)
        both = jnp.dot(jnp.concatenate([hi, lo]), z_ref[rows, 0:D], preferred_element_type=f32)
        rest = jnp.dot(hi, z_ref[rows, D : 2 * D], preferred_element_type=f32)
        part = both[:rows_here] + (both[rows_here:] + rest)
        total = part if total is None else total + part
    acc_ref[...] += total

    @pl.when(k == STEPS // WIDE - 1)
    def _():
        for i, out_ref in enumerate(out_refs):
            out_ref[0:PER, :] = acc_ref[i * PER : (i + 1) * PER, :]
            out_ref[PER:BLOCK, :] = jnp.broadcast_to(logs_ref[...], (BLOCK - PER, D))


def gradients(slots, sums, e, z, partner, weights=None):
    count = len(slots)
    first = weights is None
    vmem = pl.BlockSpec(memory_space=pltpu.VMEM)
    blocks = [jax.ShapeDtypeStruct((BLOCK, D), f32)] * count
    given, made, scratch = (), [], []
    if first:
        made = [
            jax.ShapeDtypeStruct((C, 128), f32),
            jax.ShapeDtypeStruct((STEPS, 1, SPAN), f32),
            jax.ShapeDtypeStruct((1, D), f32),
        ]
        scratch = [pltpu.VMEM((R_BLOCKS, 8, 256), f32)]
    else:
        given = weights
    size = count * PER * R
    return pl.pallas_call(
        functools.partial(gradient_kernel, slots, first),
        grid=(STEPS // WIDE,),
        in_specs=[vmem]
        + [pl.BlockSpec((WIDE * TILES, PER, LANES), lambda k, i=i: (k, i, 0)) for i in slots]
        + [pl.BlockSpec((WIDE * SPAN, 2 * D), lambda k: (k, 0)), pl.BlockSpec((WIDE, 1, SPAN), lambda k: (k, 0, 0))]
        + [vmem] * len(given),
        out_specs=[vmem] * (count + len(made)),
        out_shape=blocks + made,
        scratch_shapes=[pltpu.VMEM((count * PER, D), f32)] + scratch,
        compiler_params=pltpu.CompilerParams(vmem_limit_bytes=40 << 20),
        cost_estimate=pl.CostEstimate(flops=6 * size * D, bytes_accessed=4 * size, transcendentals=0),
    )(sums, *[e] * count, z, partner, *given)


def finish_kernel(z_ref, *refs):
    *term_refs, mean_ref, grad_ref = refs
    total = term_refs[0][...]
    for ref in term_refs[1:]:
        total = total + ref[...]
    mean_ref[0, 0] = jnp.sum(total[PER : PER + 1, 0:1]) / VIEWS
    z = z_ref[...]
    scale = lax.rsqrt(jnp.sum(z * z, axis=-1, keepdims=True) + 1e-06)
    z = z * scale
    dz = total[0:PER, :] * (1.0 / TEMPERATURE)
    grad_ref[...] = (dz - z * jnp.sum(z * dz, axis=-1, keepdims=True)) * scale


def finish(z, *terms):
    return pl.pallas_call(
        finish_kernel,
        in_specs=[pl.BlockSpec(memory_space=pltpu.VMEM)] * (1 + len(terms)),
        out_specs=[pl.BlockSpec(memory_space=pltpu.SMEM), pl.BlockSpec(memory_space=pltpu.VMEM)],
        out_shape=[jax.ShapeDtypeStruct((1, 1), f32), jax.ShapeDtypeStruct((PER, D), f32)],
        compiler_params=pltpu.CompilerParams(vmem_limit_bytes=16 << 20),
    )(z, *terms)


def pack_kernel(z_ref, partner_ref, out_ref):
    out_ref[0:PER, :] = z_ref[...]
    out_ref[PER:BLOCK, :] = jnp.zeros((BLOCK - PER, D), f32)
    out_ref[PER : PER + 1, 0:PER] = partner_ref[...].reshape(1, PER).astype(f32)


def pack(z, partner):
    return pl.pallas_call(
        pack_kernel,
        in_specs=[pl.BlockSpec(memory_space=pltpu.VMEM)] * 2,
        out_specs=pl.BlockSpec(memory_space=pltpu.VMEM),
        out_shape=jax.ShapeDtypeStruct((BLOCK, D), f32),
        compiler_params=pltpu.CompilerParams(vmem_limit_bytes=16 << 20),
    )(z, partner)


SWAP = [(0, 1), (1, 0)]
UP = [(i, (i + 1) % 4) for i in range(4)]
DOWN = [(i, (i + 3) % 4) for i in range(4)]


def over_y(down, up, across):
    across = lax.ppermute(across, "y", [(i, (i + 2) % 4) for i in range(4)])
    return across, lax.ppermute(down, "y", DOWN), lax.ppermute(up, "y", UP)


def shards(projections, partner):
    here = (pltpu.with_memory_space_constraint(v, pltpu.HBM) for v in (projections, partner))
    z, block = lax.optimization_barrier((projections, pack(*here)))
    a = lax.ppermute(z, "zl", SWAP)
    b = lax.ppermute(block, "zh", SWAP)
    c0 = jnp.concatenate([a, block[:PER]])
    c1, c2 = lax.ppermute(c0, "y", UP), lax.ppermute(c0, "y", DOWN)
    c3z, c3a = lax.ppermute(c1[PER:], "y", UP), lax.ppermute(c2[:PER], "y", DOWN)
    r0 = jnp.concatenate([b, block])
    r1, r2 = lax.ppermute(r0, "x", UP), lax.ppermute(r0, "x", DOWN)
    r3z, r3b = lax.ppermute(r1[BLOCK:], "x", UP), lax.ppermute(r2[:BLOCK], "x", DOWN)
    swap = lambda r: lax.ppermute(r, "core", SWAP)
    columns = (z, c1[PER:], c2[PER:], c3z, a, c1[:PER], c2[:PER], c3a)
    rows = [(r[BLOCK:], r[:BLOCK], q[BLOCK:], q[:BLOCK]) for r, q in ((r, swap(r)) for r in (r0, r1, r2))]
    carried = scores(0, rows[0], columns)
    carried = scores(1, rows[1], carried=carried)
    e, zr, partners, sums = scores(2, (*rows[2], r3z, r3b, swap(r3z), swap(r3b)), carried=carried)
    sums = lax.all_to_all(sums, ALL, 0, 0, tiled=True)
    e, zr, partners = (pltpu.with_memory_space_constraint(v, pltpu.HBM) for v in (e, zr, partners))
    here, *away, uc, ur, logs = gradients((4, 5, 6, 7), sums, e, zr, partners)
    other = sum(over_y(*away), here)
    away = gradients((1, 2, 3), logs, e, zr, partners, (uc, ur))
    logs, other = lax.optimization_barrier((logs, other))
    (here,) = gradients((0,), logs, e, zr, partners, (uc, ur))
    mean_objective, grad = finish(z, here, *over_y(*away), lax.ppermute(other, "zl", SWAP))
    return mean_objective[0, 0], grad


def solution(mesh):
    fine = Mesh(mesh.devices.reshape(4, 2, 4, 2, 2), ALL)
    placed = (P(ALL, None), P(ALL))
    return jax.shard_map(
        shards, mesh=fine, in_specs=placed, out_specs=(P(), P(ALL, None)), check_vma=False
    )
```

```python
import functools

import jax
import jax.numpy as jnp
from jax import lax
from jax.experimental import pallas as pl
from jax.experimental.pallas import tpu as pltpu
from jax.sharding import Mesh, PartitionSpec as P

f32, bf16 = jnp.float32, jnp.bfloat16
PER = 192
D = 256
VIEWS = 24576
C_BLOCKS = 8
R_BLOCKS = 16
C = C_BLOCKS * PER
R = R_BLOCKS * PER
SPAN = 768
STEPS = R // SPAN
LANES = 256
TILES = SPAN // LANES
WIDE = 2
BLOCK = 200
PAIR = PER + BLOCK
TEMPERATURE = 0.1
LOG2E = 1.4426950408889634
LN2 = 0.6931471805599453
NT = (((1,), (1,)), ((), ()))
ROW = ("y", "zl")
COL = ("x", "zh", "core")
ALL = ROW + COL


def unit(rows):
    return rows * lax.rsqrt(jnp.sum(rows * rows, axis=-1, keepdims=True) + 1e-06)


def halves(a):
    hi = a.astype(bf16)
    return hi, (a - hi.astype(f32)).astype(bf16)


def places():
    y, zl, x, zh, core = (lax.axis_index(a) for a in ALL)
    found = []
    for dz in (0, 1):
        for dy in (0, -1, 1, 2):
            found.append((y + 4 + dy) % 4 * 2 + (zl + dz) % 2)
    for dx in (0, -1, 1, 2):
        for dcore in (0, 1):
            for dz in (0, 1):
                found.append(((x + 4 + dx) % 4 * 2 + (zh + dz) % 2) * 2 + (core + dcore) % 2)
    return found + [(x * 2 + zh) * 2 + core]


def score_kernel(start, steps, *refs):
    place = places()
    first, last = start == 0, start + steps == STEPS
    if first:
        columns, refs = refs[:C_BLOCKS], refs[C_BLOCKS:]
        blocks, refs = refs[: 4 * steps], refs[4 * steps :]
        e_ref, zr_ref, partner_ref, rsum_ref, pos_ref, cacc_ref, a_ref, cid_ref, b_ref = refs
    else:
        blocks, refs = refs[: 4 * steps], refs[4 * steps :]
        a_ref, cid_ref, pos_in_ref, cacc_in_ref = refs[:4]
        refs = refs[7:]
        if last:
            earlier_ref, refs = refs[0], refs[1:]
            e_ref, zr_ref, partner_ref, send_ref, b_ref, rsum_ref, pos_ref, cacc_ref, rows_ref = refs
        else:
            e_ref, zr_ref, partner_ref, rsum_ref, pos_ref, cacc_ref, b_ref = refs
    j = pl.program_id(0)

    @pl.when(j == 0)
    def _():
        if first:
            cacc_ref[...] = jnp.zeros_like(cacc_ref)
            pos_ref[...] = jnp.zeros_like(pos_ref)
            for s, ref in enumerate(columns):
                rows = pl.ds(s * PER, PER)
                hi, lo = halves(unit(ref[...]) * (LOG2E / TEMPERATURE))
                a_ref[rows, 0:D] = hi
                a_ref[rows, D : 2 * D] = lo
                a_ref[rows, 2 * D : 3 * D] = hi
                start = (place[s] * R_BLOCKS + place[24]) * PER
                cid_ref[rows, :] = (start + lax.broadcasted_iota(jnp.int32, (PER, 128), 0)).astype(f32)
        else:
            cacc_ref[...] = cacc_in_ref[...]
            pos_ref[...] = pos_in_ref[...]

    for step in range(len(blocks) // 4):

        @pl.when(j == step * TILES)
        def _():
            for b, ref in enumerate(blocks[4 * step : 4 * step + 4]):
                hi, lo = halves(unit(ref[0:PER, :]))
                rows = pl.ds(b * PER, PER)
                b_ref[rows, 0:D] = hi
                b_ref[rows, D : 2 * D] = hi
                b_ref[rows, 2 * D : 3 * D] = lo
                zr_ref[rows, 0:D] = hi
                zr_ref[rows, D : 2 * D] = lo
                partner_ref[0, :, b * PER : (b + 1) * PER] = ref[PER : PER + 1, 0:PER]

    cid = cid_ref[...]
    tile = lax.rem(j, TILES) * LANES
    s = lax.dot_general(
        a_ref[...], b_ref[pl.ds(pl.multiple_of(tile, LANES), LANES), :], NT, preferred_element_type=f32
    )
    row_total = None
    for h in range(LANES // 128):
        lanes = pl.ds(pl.multiple_of(tile + h * 128, 128), 128)
        part = s[:, h * 128 : (h + 1) * 128]
        e = jnp.exp2(part)
        if first:
            i = lax.broadcasted_iota(jnp.int32, (PER, 128), 0)
            i2 = lax.broadcasted_iota(jnp.int32, (PER, 128), 1) + h * 128
            e = jnp.concatenate([jnp.where((i == i2) & (j == 0), 0.0, e[:PER]), e[PER:]])
        hit = jnp.where(cid == partner_ref[0, :, lanes], part, 0.0)
        e_ref[0, :, h * 128 : (h + 1) * 128] = e
        rsum_ref[j // TILES, :, lanes] = jnp.sum(e, axis=0, keepdims=True)
        pos_ref[...] += jnp.sum(hit.reshape(C // 8, 8, 128), axis=0)
        row_total = e if row_total is None else row_total + e
    cacc_ref[...] += row_total

    if last:

        @pl.when(j == pl.num_programs(0) - 1)
        def _():
            csum = lax.dot_general(
                jnp.ones((8, 128), f32), cacc_ref[...], NT, precision=lax.Precision.HIGHEST, preferred_element_type=f32
            )
            positives = jnp.full((R_BLOCKS, 256 - PER), jnp.sum(pos_ref[...]), f32)
            for s in range(R_BLOCKS):
                step, b = divmod(s, 4)
                sums = earlier_ref[step] if step < start else rsum_ref[step - start]
                rows_ref[place[C_BLOCKS + s], 0:1, 0:PER] = sums[:, b * PER : (b + 1) * PER]
            of_rows = jnp.concatenate([rows_ref[c, 0:1, 0:PER] for c in range(R_BLOCKS)])
            for s in range(C_BLOCKS):
                rows = pl.ds(place[s] * R_BLOCKS, R_BLOCKS)
                mine = jnp.broadcast_to(csum[0:1, s * PER : (s + 1) * PER], (R_BLOCKS, PER))
                send_ref[rows, 0, :] = jnp.concatenate([mine, positives, of_rows, positives], axis=1)


def scores(start, blocks, columns=None, carried=None):
    vmem = pl.BlockSpec(memory_space=pltpu.VMEM)
    steps = len(blocks) // 4
    first, last = start == 0, start + steps == STEPS
    shared = [
        pltpu.HBM((R // LANES, C, LANES), f32),
        pltpu.HBM((R, 2 * D), bf16),
        pltpu.HBM((STEPS, 1, SPAN), f32),
    ]
    shared_specs = [
        pl.BlockSpec((1, C, LANES), lambda j: (start * TILES + j, 0, 0)),
        pl.BlockSpec((SPAN, 2 * D), lambda j: (start + j // TILES, 0)),
        pl.BlockSpec((1, 1, SPAN), lambda j: (start + j // TILES, 0, 0)),
    ]
    sums = [pltpu.VMEM((steps, 1, SPAN), f32), pltpu.VMEM((8, 128), f32), pltpu.VMEM((C, 128), f32)]
    scratch = [pltpu.VMEM((SPAN, 3 * D), bf16)]
    if first:
        given, in_specs, aliases = (*columns, *blocks), [vmem] * (C_BLOCKS + len(blocks)), {}
        made = sums + [pltpu.VMEM((C, 3 * D), bf16), pltpu.VMEM((C, 128), f32)]
    else:
        e, zr, partners, rsums, pos, cacc, a, cid = carried
        keep = lambda v: pltpu.with_memory_space_constraint(v, pltpu.VMEM)
        given = (*blocks, *(keep(v) for v in (a, cid, pos, cacc)), e, zr, partners)
        n = len(given) - 3
        in_specs = [vmem] * n + [pl.BlockSpec(memory_space=pl.ANY)] * 3
        aliases = {n: 0, n + 1: 1, n + 2: 2}
        made = sums
        if last:
            given, in_specs = (*given, *(keep(v) for v in rsums)), in_specs + [vmem] * len(rsums)
            made = [jax.ShapeDtypeStruct((C_BLOCKS * R_BLOCKS, 1, 512), f32)]
            scratch += sums + [pltpu.VMEM((R_BLOCKS, 8, 256), f32)]
    size = C * SPAN * steps
    out = pl.pallas_call(
        functools.partial(score_kernel, start, steps),
        grid=(steps * TILES,),
        in_specs=in_specs,
        out_specs=shared_specs + [vmem] * len(made),
        out_shape=shared + made,
        scratch_shapes=scratch,
        input_output_aliases=aliases,
        compiler_params=pltpu.CompilerParams(vmem_limit_bytes=40 << 20),
        cost_estimate=pl.CostEstimate(flops=6 * size * D, bytes_accessed=4 * size, transcendentals=size),
    )(*given)
    if last:
        return out
    e, zr, partners, rsum, pos, cacc = out[:6]
    if first:
        return e, zr, partners, [rsum], pos, cacc, *out[6:]
    return e, zr, partners, [*rsums, rsum], pos, cacc, a, cid


def gradient_kernel(slots, first, sums_ref, *refs):
    count = len(slots)
    e_refs, (z_ref, partner_ref), refs = refs[:count], refs[count : count + 2], refs[count + 2 :]
    if not first:
        (uc_ref, ur_ref), logs_ref, refs = refs[:2], sums_ref, refs[2:]
    out_refs, refs = refs[:count], refs[count:]
    if first:
        uc_ref, ur_ref, logs_ref, acc_ref, total_ref = refs
    else:
        (acc_ref,) = refs
    place = places()
    k = pl.program_id(0)
    rows_here = count * PER

    @pl.when(k == 0)
    def _():
        acc_ref[...] = jnp.zeros_like(acc_ref)
        if first:
            total = sums_ref[0:R_BLOCKS, 0, :]
            for r in range(1, C_BLOCKS):
                total = total + sums_ref[r * R_BLOCKS : (r + 1) * R_BLOCKS, 0, :]
            for c in range(R_BLOCKS):
                total_ref[c, 0:1, :] = total[c : c + 1, 0:256]
            logs = jnp.sum(jnp.log(total[:, 0:PER]))
            positives = jnp.sum(total[:, PER : PER + 1]) * LN2
            logs_ref[...] = jnp.full(logs_ref.shape, logs - positives / C_BLOCKS, f32)
            for s in range(R_BLOCKS):
                step, b = divmod(s, 4)
                found = total_ref[place[C_BLOCKS + s], 0:1, 0:PER]
                ur_ref[step, :, b * PER : (b + 1) * PER] = 1.0 / found
            for s in range(C_BLOCKS):
                mine = sums_ref[pl.ds(place[s] * R_BLOCKS, R_BLOCKS), 0, 256 : 256 + PER]
                found = 1.0 / jnp.sum(mine, axis=0, keepdims=True)
                uc_ref[s * PER : (s + 1) * PER, :] = jnp.broadcast_to(found, (128, PER)).T

    uc = jnp.concatenate([uc_ref[i * PER : (i + 1) * PER, :] for i in slots])
    ids = lax.broadcasted_iota(jnp.int32, (PER, 128), 0)
    ids = jnp.concatenate([ids + (place[i] * R_BLOCKS + place[24]) * PER for i in slots]).astype(f32)
    total = None
    for c in range(0, WIDE * SPAN, 256):
        his, los = [], []
        for h in range(c, c + 256, 128):
            part, lanes = h // SPAN, pl.ds(h % SPAN, 128)
            e = jnp.concatenate([e_ref[c // 256, :, h - c : h - c + 128] for e_ref in e_refs])
            g = e * (uc + ur_ref[WIDE * k + part, :, lanes])
            g = g - jnp.where(ids == partner_ref[part, :, lanes], 2.0, 0.0)
            hi, lo = halves(g)
            his.append(hi)
            los.append(lo)
        hi, lo = jnp.concatenate(his, axis=1), jnp.concatenate(los, axis=1)
        rows = pl.ds(c, 256)
        both = jnp.dot(jnp.concatenate([hi, lo]), z_ref[rows, 0:D], preferred_element_type=f32)
        rest = jnp.dot(hi, z_ref[rows, D : 2 * D], preferred_element_type=f32)
        part = both[:rows_here] + (both[rows_here:] + rest)
        total = part if total is None else total + part
    acc_ref[...] += total

    @pl.when(k == STEPS // WIDE - 1)
    def _():
        for i, out_ref in enumerate(out_refs):
            out_ref[0:PER, :] = acc_ref[i * PER : (i + 1) * PER, :]
            out_ref[PER:BLOCK, :] = jnp.broadcast_to(logs_ref[...], (BLOCK - PER, D))


def gradients(slots, sums, e, z, partner, weights=None):
    count = len(slots)
    first = weights is None
    vmem = pl.BlockSpec(memory_space=pltpu.VMEM)
    blocks = [jax.ShapeDtypeStruct((BLOCK, D), f32)] * count
    given, made, scratch = (), [], []
    if first:
        made = [
            jax.ShapeDtypeStruct((C, 128), f32),
            jax.ShapeDtypeStruct((STEPS, 1, SPAN), f32),
            jax.ShapeDtypeStruct((1, D), f32),
        ]
        scratch = [pltpu.VMEM((R_BLOCKS, 8, 256), f32)]
    else:
        given = weights
    size = count * PER * R
    return pl.pallas_call(
        functools.partial(gradient_kernel, slots, first),
        grid=(STEPS // WIDE,),
        in_specs=[vmem]
        + [pl.BlockSpec((WIDE * TILES, PER, LANES), lambda k, i=i: (k, i, 0)) for i in slots]
        + [pl.BlockSpec((WIDE * SPAN, 2 * D), lambda k: (k, 0)), pl.BlockSpec((WIDE, 1, SPAN), lambda k: (k, 0, 0))]
        + [vmem] * len(given),
        out_specs=[vmem] * (count + len(made)),
        out_shape=blocks + made,
        scratch_shapes=[pltpu.VMEM((count * PER, D), f32)] + scratch,
        compiler_params=pltpu.CompilerParams(vmem_limit_bytes=40 << 20),
        cost_estimate=pl.CostEstimate(flops=6 * size * D, bytes_accessed=4 * size, transcendentals=0),
    )(sums, *[e] * count, z, partner, *given)


def finish_kernel(z_ref, *refs):
    *term_refs, mean_ref, grad_ref = refs
    total = term_refs[0][...]
    for ref in term_refs[1:]:
        total = total + ref[...]
    mean_ref[0, 0] = jnp.sum(total[PER : PER + 1, 0:1]) / VIEWS
    z = z_ref[...]
    scale = lax.rsqrt(jnp.sum(z * z, axis=-1, keepdims=True) + 1e-06)
    z = z * scale
    dz = total[0:PER, :] * (1.0 / TEMPERATURE)
    grad_ref[...] = (dz - z * jnp.sum(z * dz, axis=-1, keepdims=True)) * scale


def finish(z, *terms):
    return pl.pallas_call(
        finish_kernel,
        in_specs=[pl.BlockSpec(memory_space=pltpu.VMEM)] * (1 + len(terms)),
        out_specs=[pl.BlockSpec(memory_space=pltpu.SMEM), pl.BlockSpec(memory_space=pltpu.VMEM)],
        out_shape=[jax.ShapeDtypeStruct((1, 1), f32), jax.ShapeDtypeStruct((PER, D), f32)],
        compiler_params=pltpu.CompilerParams(vmem_limit_bytes=16 << 20),
    )(z, *terms)


def pack_kernel(z_ref, partner_ref, out_ref):
    out_ref[0:PER, :] = z_ref[...]
    out_ref[PER:BLOCK, :] = jnp.zeros((BLOCK - PER, D), f32)
    out_ref[PER : PER + 1, 0:PER] = partner_ref[...].reshape(1, PER).astype(f32)


def pack(z, partner):
    return pl.pallas_call(
        pack_kernel,
        in_specs=[pl.BlockSpec(memory_space=pltpu.VMEM)] * 2,
        out_specs=pl.BlockSpec(memory_space=pltpu.VMEM),
        out_shape=jax.ShapeDtypeStruct((BLOCK, D), f32),
        compiler_params=pltpu.CompilerParams(vmem_limit_bytes=16 << 20),
    )(z, partner)


SWAP = [(0, 1), (1, 0)]
UP = [(i, (i + 1) % 4) for i in range(4)]
DOWN = [(i, (i + 3) % 4) for i in range(4)]


def over_y(down, up, across):
    across = lax.ppermute(across, "y", [(i, (i + 2) % 4) for i in range(4)])
    return across, lax.ppermute(down, "y", DOWN), lax.ppermute(up, "y", UP)


def shards(projections, partner):
    here = (pltpu.with_memory_space_constraint(v, pltpu.HBM) for v in (projections, partner))
    z, block = lax.optimization_barrier((projections, pack(*here)))
    a = lax.ppermute(z, "zl", SWAP)
    b = lax.ppermute(block, "zh", SWAP)
    c0 = jnp.concatenate([a, block[:PER]])
    c1, c2 = lax.ppermute(c0, "y", UP), lax.ppermute(c0, "y", DOWN)
    c3z, c3a = lax.ppermute(c1[PER:], "y", UP), lax.ppermute(c2[:PER], "y", DOWN)
    r0 = jnp.concatenate([b, block])
    r1, r2 = lax.ppermute(r0, "x", UP), lax.ppermute(r0, "x", DOWN)
    r3z, r3b = lax.ppermute(r1[BLOCK:], "x", UP), lax.ppermute(r2[:BLOCK], "x", DOWN)
    swap = lambda r: lax.ppermute(r, "core", SWAP)
    columns = (z, c1[PER:], c2[PER:], c3z, a, c1[:PER], c2[:PER], c3a)
    pieces = lambda r, q: (r[BLOCK:], r[:BLOCK], q[BLOCK:], q[:BLOCK])
    s0, s1, s2 = swap(r0), swap(r1), swap(r2)
    carried = scores(0, (*pieces(r0, s0), *pieces(r1, s1)), columns)
    r3z, r3b, carried = lax.optimization_barrier((r3z, r3b, carried))
    e, zr, partners, sums = scores(2, (*pieces(r2, s2), r3z, r3b, swap(r3z), swap(r3b)), carried=carried)
    sums = lax.all_to_all(sums, ALL, 0, 0, tiled=True)
    e, zr, partners = (pltpu.with_memory_space_constraint(v, pltpu.HBM) for v in (e, zr, partners))
    here, *away, uc, ur, logs = gradients((4, 5, 6, 7), sums, e, zr, partners)
    other = sum(over_y(*away), here)
    away = gradients((1, 2, 3), logs, e, zr, partners, (uc, ur))
    logs, other = lax.optimization_barrier((logs, other))
    (here,) = gradients((0,), logs, e, zr, partners, (uc, ur))
    mean_objective, grad = finish(z, here, *over_y(*away), lax.ppermute(other, "zl", SWAP))
    return mean_objective[0, 0], grad


def solution(mesh):
    fine = Mesh(mesh.devices.reshape(4, 2, 4, 2, 2), ALL)
    placed = (P(ALL, None), P(ALL))
    return jax.shard_map(
        shards, mesh=fine, in_specs=placed, out_specs=(P(), P(ALL, None)), check_vma=False
    )
```

```python
import functools

import jax
import jax.numpy as jnp
from jax import lax
from jax.experimental import pallas as pl
from jax.experimental.pallas import tpu as pltpu
from jax.sharding import Mesh, PartitionSpec as P

f32, bf16 = jnp.float32, jnp.bfloat16
PER = 192
D = 256
VIEWS = 24576
C_BLOCKS = 8
R_BLOCKS = 16
C = C_BLOCKS * PER
R = R_BLOCKS * PER
SPAN = 768
STEPS = R // SPAN
LANES = 256
TILES = SPAN // LANES
WIDE = 2
BLOCK = 200
PAIR = PER + BLOCK
TEMPERATURE = 0.1
LOG2E = 1.4426950408889634
LN2 = 0.6931471805599453
NT = (((1,), (1,)), ((), ()))
ROW = ("y", "zl")
COL = ("x", "zh", "core")
ALL = ROW + COL


def unit(rows):
    return rows * lax.rsqrt(jnp.sum(rows * rows, axis=-1, keepdims=True) + 1e-06)


def halves(a):
    hi = a.astype(bf16)
    return hi, (a - hi.astype(f32)).astype(bf16)


def places():
    y, zl, x, zh, core = (lax.axis_index(a) for a in ALL)
    found = []
    for dz in (0, 1):
        for dy in (0, -1, 1, 2):
            found.append((y + 4 + dy) % 4 * 2 + (zl + dz) % 2)
    for dx in (0, -1, 1, 2):
        for dcore in (0, 1):
            for dz in (0, 1):
                found.append(((x + 4 + dx) % 4 * 2 + (zh + dz) % 2) * 2 + (core + dcore) % 2)
    return found + [(x * 2 + zh) * 2 + core]


def score_kernel(start, steps, *refs):
    place = places()
    first, last = start == 0, start + steps == STEPS
    if first:
        columns, refs = refs[:C_BLOCKS], refs[C_BLOCKS:]
        blocks, refs = refs[: 4 * steps], refs[4 * steps :]
        e_ref, zr_ref, partner_ref, rsum_ref, pos_ref, cacc_ref, a_ref, cid_ref, b_ref = refs
    else:
        blocks, refs = refs[: 4 * steps], refs[4 * steps :]
        a_ref, cid_ref, pos_in_ref, cacc_in_ref = refs[:4]
        refs = refs[7:]
        if last:
            *earlier, refs = refs[0], refs[1], refs[2:]
            e_ref, zr_ref, partner_ref, send_ref, b_ref, rsum_ref, pos_ref, cacc_ref, rows_ref = refs
        else:
            e_ref, zr_ref, partner_ref, rsum_ref, pos_ref, cacc_ref, b_ref = refs
    j = pl.program_id(0)

    @pl.when(j == 0)
    def _():
        if first:
            cacc_ref[...] = jnp.zeros_like(cacc_ref)
            pos_ref[...] = jnp.zeros_like(pos_ref)
            for s, ref in enumerate(columns):
                rows = pl.ds(s * PER, PER)
                hi, lo = halves(unit(ref[...]) * (LOG2E / TEMPERATURE))
                a_ref[rows, 0:D] = hi
                a_ref[rows, D : 2 * D] = lo
                a_ref[rows, 2 * D : 3 * D] = hi
                start = (place[s] * R_BLOCKS + place[24]) * PER
                cid_ref[rows, :] = (start + lax.broadcasted_iota(jnp.int32, (PER, 128), 0)).astype(f32)
        else:
            cacc_ref[...] = cacc_in_ref[...]
            pos_ref[...] = pos_in_ref[...]

    for step in range(len(blocks) // 4):

        @pl.when(j == step * TILES)
        def _():
            for b, ref in enumerate(blocks[4 * step : 4 * step + 4]):
                hi, lo = halves(unit(ref[0:PER, :]))
                rows = pl.ds(b * PER, PER)
                b_ref[rows, 0:D] = hi
                b_ref[rows, D : 2 * D] = hi
                b_ref[rows, 2 * D : 3 * D] = lo
                zr_ref[rows, 0:D] = hi
                zr_ref[rows, D : 2 * D] = lo
                partner_ref[0, :, b * PER : (b + 1) * PER] = ref[PER : PER + 1, 0:PER]

    cid = cid_ref[...]
    tile = lax.rem(j, TILES) * LANES
    s = lax.dot_general(
        a_ref[...], b_ref[pl.ds(pl.multiple_of(tile, LANES), LANES), :], NT, preferred_element_type=f32
    )
    row_total = None
    for h in range(LANES // 128):
        lanes = pl.ds(pl.multiple_of(tile + h * 128, 128), 128)
        part = s[:, h * 128 : (h + 1) * 128]
        e = jnp.exp2(part)
        if first:
            i = lax.broadcasted_iota(jnp.int32, (PER, 128), 0)
            i2 = lax.broadcasted_iota(jnp.int32, (PER, 128), 1) + h * 128
            e = jnp.concatenate([jnp.where((i == i2) & (j == 0), 0.0, e[:PER]), e[PER:]])
        hit = jnp.where(cid == partner_ref[0, :, lanes], part, 0.0)
        e_ref[0, :, h * 128 : (h + 1) * 128] = e
        rsum_ref[j // TILES, :, lanes] = jnp.sum(e, axis=0, keepdims=True)
        pos_ref[...] += jnp.sum(hit.reshape(C // 8, 8, 128), axis=0)
        row_total = e if row_total is None else row_total + e
    cacc_ref[...] += row_total

    if last:

        @pl.when(j == pl.num_programs(0) - 1)
        def _():
            csum = lax.dot_general(
                jnp.ones((8, 128), f32), cacc_ref[...], NT, precision=lax.Precision.HIGHEST, preferred_element_type=f32
            )
            positives = jnp.full((R_BLOCKS, 256 - PER), jnp.sum(pos_ref[...]), f32)
            for s in range(R_BLOCKS):
                step, b = divmod(s, 4)
                sums = (earlier[0][0], earlier[0][1], earlier[1][0], rsum_ref[0])[step]
                rows_ref[place[C_BLOCKS + s], 0:1, 0:PER] = sums[:, b * PER : (b + 1) * PER]
            of_rows = jnp.concatenate([rows_ref[c, 0:1, 0:PER] for c in range(R_BLOCKS)])
            for s in range(C_BLOCKS):
                rows = pl.ds(place[s] * R_BLOCKS, R_BLOCKS)
                mine = jnp.broadcast_to(csum[0:1, s * PER : (s + 1) * PER], (R_BLOCKS, PER))
                send_ref[rows, 0, :] = jnp.concatenate([mine, positives, of_rows, positives], axis=1)


def scores(start, blocks, columns=None, carried=None):
    vmem = pl.BlockSpec(memory_space=pltpu.VMEM)
    steps = len(blocks) // 4
    first, last = start == 0, start + steps == STEPS
    shared = [
        pltpu.HBM((R // LANES, C, LANES), f32),
        pltpu.HBM((R, 2 * D), bf16),
        pltpu.HBM((STEPS, 1, SPAN), f32),
    ]
    shared_specs = [
        pl.BlockSpec((1, C, LANES), lambda j: (start * TILES + j, 0, 0)),
        pl.BlockSpec((SPAN, 2 * D), lambda j: (start + j // TILES, 0)),
        pl.BlockSpec((1, 1, SPAN), lambda j: (start + j // TILES, 0, 0)),
    ]
    sums = [pltpu.VMEM((steps, 1, SPAN), f32), pltpu.VMEM((8, 128), f32), pltpu.VMEM((C, 128), f32)]
    scratch = [pltpu.VMEM((SPAN, 3 * D), bf16)]
    if first:
        given, in_specs, aliases = (*columns, *blocks), [vmem] * (C_BLOCKS + len(blocks)), {}
        made = sums + [pltpu.VMEM((C, 3 * D), bf16), pltpu.VMEM((C, 128), f32)]
    else:
        e, zr, partners, rsums, pos, cacc, a, cid = carried
        keep = lambda v: pltpu.with_memory_space_constraint(v, pltpu.VMEM)
        given = (*blocks, *(keep(v) for v in (a, cid, pos, cacc)), e, zr, partners)
        n = len(given) - 3
        in_specs = [vmem] * n + [pl.BlockSpec(memory_space=pl.ANY)] * 3
        aliases = {n: 0, n + 1: 1, n + 2: 2}
        made = sums
        if last:
            given, in_specs = (*given, *(keep(v) for v in rsums)), in_specs + [vmem] * len(rsums)
            made = [jax.ShapeDtypeStruct((C_BLOCKS * R_BLOCKS, 1, 512), f32)]
            scratch += sums + [pltpu.VMEM((R_BLOCKS, 8, 256), f32)]
    size = C * SPAN * steps
    out = pl.pallas_call(
        functools.partial(score_kernel, start, steps),
        grid=(steps * TILES,),
        in_specs=in_specs,
        out_specs=shared_specs + [vmem] * len(made),
        out_shape=shared + made,
        scratch_shapes=scratch,
        input_output_aliases=aliases,
        compiler_params=pltpu.CompilerParams(vmem_limit_bytes=40 << 20),
        cost_estimate=pl.CostEstimate(flops=6 * size * D, bytes_accessed=4 * size, transcendentals=size),
    )(*given)
    if last:
        return out
    e, zr, partners, rsum, pos, cacc = out[:6]
    if first:
        return e, zr, partners, [rsum], pos, cacc, *out[6:]
    return e, zr, partners, [*rsums, rsum], pos, cacc, a, cid


def gradient_kernel(slots, first, sums_ref, *refs):
    count = len(slots)
    e_refs, (z_ref, partner_ref), refs = refs[:count], refs[count : count + 2], refs[count + 2 :]
    if not first:
        (uc_ref, ur_ref), logs_ref, refs = refs[:2], sums_ref, refs[2:]
    out_refs, refs = refs[:count], refs[count:]
    if first:
        uc_ref, ur_ref, logs_ref, acc_ref, total_ref = refs
    else:
        (acc_ref,) = refs
    place = places()
    k = pl.program_id(0)
    rows_here = count * PER

    @pl.when(k == 0)
    def _():
        acc_ref[...] = jnp.zeros_like(acc_ref)
        if first:
            total = sums_ref[0:R_BLOCKS, 0, :]
            for r in range(1, C_BLOCKS):
                total = total + sums_ref[r * R_BLOCKS : (r + 1) * R_BLOCKS, 0, :]
            for c in range(R_BLOCKS):
                total_ref[c, 0:1, :] = total[c : c + 1, 0:256]
            logs = jnp.sum(jnp.log(total[:, 0:PER]))
            positives = jnp.sum(total[:, PER : PER + 1]) * LN2
            logs_ref[...] = jnp.full(logs_ref.shape, logs - positives / C_BLOCKS, f32)
            for s in range(R_BLOCKS):
                step, b = divmod(s, 4)
                found = total_ref[place[C_BLOCKS + s], 0:1, 0:PER]
                ur_ref[step, :, b * PER : (b + 1) * PER] = 1.0 / found
            for s in range(C_BLOCKS):
                mine = sums_ref[pl.ds(place[s] * R_BLOCKS, R_BLOCKS), 0, 256 : 256 + PER]
                found = 1.0 / jnp.sum(mine, axis=0, keepdims=True)
                uc_ref[s * PER : (s + 1) * PER, :] = jnp.broadcast_to(found, (128, PER)).T

    uc = jnp.concatenate([uc_ref[i * PER : (i + 1) * PER, :] for i in slots])
    ids = lax.broadcasted_iota(jnp.int32, (PER, 128), 0)
    ids = jnp.concatenate([ids + (place[i] * R_BLOCKS + place[24]) * PER for i in slots]).astype(f32)
    total = None
    for c in range(0, WIDE * SPAN, 256):
        his, los = [], []
        for h in range(c, c + 256, 128):
            part, lanes = h // SPAN, pl.ds(h % SPAN, 128)
            e = jnp.concatenate([e_ref[c // 256, :, h - c : h - c + 128] for e_ref in e_refs])
            g = e * (uc + ur_ref[WIDE * k + part, :, lanes])
            g = g - jnp.where(ids == partner_ref[part, :, lanes], 2.0, 0.0)
            hi, lo = halves(g)
            his.append(hi)
            los.append(lo)
        hi, lo = jnp.concatenate(his, axis=1), jnp.concatenate(los, axis=1)
        rows = pl.ds(c, 256)
        both = jnp.dot(jnp.concatenate([hi, lo]), z_ref[rows, 0:D], preferred_element_type=f32)
        rest = jnp.dot(hi, z_ref[rows, D : 2 * D], preferred_element_type=f32)
        part = both[:rows_here] + (both[rows_here:] + rest)
        total = part if total is None else total + part
    acc_ref[...] += total

    @pl.when(k == STEPS // WIDE - 1)
    def _():
        for i, out_ref in enumerate(out_refs):
            out_ref[0:PER, :] = acc_ref[i * PER : (i + 1) * PER, :]
            out_ref[PER:BLOCK, :] = jnp.broadcast_to(logs_ref[...], (BLOCK - PER, D))


def gradients(slots, sums, e, z, partner, weights=None):
    count = len(slots)
    first = weights is None
    vmem = pl.BlockSpec(memory_space=pltpu.VMEM)
    blocks = [jax.ShapeDtypeStruct((BLOCK, D), f32)] * count
    given, made, scratch = (), [], []
    if first:
        made = [
            jax.ShapeDtypeStruct((C, 128), f32),
            jax.ShapeDtypeStruct((STEPS, 1, SPAN), f32),
            jax.ShapeDtypeStruct((1, D), f32),
        ]
        scratch = [pltpu.VMEM((R_BLOCKS, 8, 256), f32)]
    else:
        given = weights
    size = count * PER * R
    return pl.pallas_call(
        functools.partial(gradient_kernel, slots, first),
        grid=(STEPS // WIDE,),
        in_specs=[vmem]
        + [pl.BlockSpec((WIDE * TILES, PER, LANES), lambda k, i=i: (k, i, 0)) for i in slots]
        + [pl.BlockSpec((WIDE * SPAN, 2 * D), lambda k: (k, 0)), pl.BlockSpec((WIDE, 1, SPAN), lambda k: (k, 0, 0))]
        + [vmem] * len(given),
        out_specs=[vmem] * (count + len(made)),
        out_shape=blocks + made,
        scratch_shapes=[pltpu.VMEM((count * PER, D), f32)] + scratch,
        compiler_params=pltpu.CompilerParams(vmem_limit_bytes=40 << 20),
        cost_estimate=pl.CostEstimate(flops=6 * size * D, bytes_accessed=4 * size, transcendentals=0),
    )(sums, *[e] * count, z, partner, *given)


def finish_kernel(z_ref, *refs):
    *term_refs, mean_ref, grad_ref = refs
    total = term_refs[0][...]
    for ref in term_refs[1:]:
        total = total + ref[...]
    mean_ref[0, 0] = jnp.sum(total[PER : PER + 1, 0:1]) / VIEWS
    z = z_ref[...]
    scale = lax.rsqrt(jnp.sum(z * z, axis=-1, keepdims=True) + 1e-06)
    z = z * scale
    dz = total[0:PER, :] * (1.0 / TEMPERATURE)
    grad_ref[...] = (dz - z * jnp.sum(z * dz, axis=-1, keepdims=True)) * scale


def finish(z, *terms):
    return pl.pallas_call(
        finish_kernel,
        in_specs=[pl.BlockSpec(memory_space=pltpu.VMEM)] * (1 + len(terms)),
        out_specs=[pl.BlockSpec(memory_space=pltpu.SMEM), pl.BlockSpec(memory_space=pltpu.VMEM)],
        out_shape=[jax.ShapeDtypeStruct((1, 1), f32), jax.ShapeDtypeStruct((PER, D), f32)],
        compiler_params=pltpu.CompilerParams(vmem_limit_bytes=16 << 20),
    )(z, *terms)


def pack_kernel(z_ref, partner_ref, out_ref):
    out_ref[0:PER, :] = z_ref[...]
    out_ref[PER:BLOCK, :] = jnp.zeros((BLOCK - PER, D), f32)
    out_ref[PER : PER + 1, 0:PER] = partner_ref[...].reshape(1, PER).astype(f32)


def pack(z, partner):
    return pl.pallas_call(
        pack_kernel,
        in_specs=[pl.BlockSpec(memory_space=pltpu.VMEM)] * 2,
        out_specs=pl.BlockSpec(memory_space=pltpu.VMEM),
        out_shape=jax.ShapeDtypeStruct((BLOCK, D), f32),
        compiler_params=pltpu.CompilerParams(vmem_limit_bytes=16 << 20),
    )(z, partner)


SWAP = [(0, 1), (1, 0)]
UP = [(i, (i + 1) % 4) for i in range(4)]
DOWN = [(i, (i + 3) % 4) for i in range(4)]


def over_y(down, up, across):
    across = lax.ppermute(across, "y", [(i, (i + 2) % 4) for i in range(4)])
    return across, lax.ppermute(down, "y", DOWN), lax.ppermute(up, "y", UP)


def shards(projections, partner):
    here = (pltpu.with_memory_space_constraint(v, pltpu.HBM) for v in (projections, partner))
    z, block = lax.optimization_barrier((projections, pack(*here)))
    a = lax.ppermute(z, "zl", SWAP)
    b = lax.ppermute(block, "zh", SWAP)
    c0 = jnp.concatenate([a, block[:PER]])
    c1, c2 = lax.ppermute(c0, "y", UP), lax.ppermute(c0, "y", DOWN)
    c3z, c3a = lax.ppermute(c1[PER:], "y", UP), lax.ppermute(c2[:PER], "y", DOWN)
    r0 = jnp.concatenate([b, block])
    r1, r2 = lax.ppermute(r0, "x", UP), lax.ppermute(r0, "x", DOWN)
    r3z, r3b = lax.ppermute(r1[BLOCK:], "x", UP), lax.ppermute(r2[:BLOCK], "x", DOWN)
    swap = lambda r: lax.ppermute(r, "core", SWAP)
    columns = (z, c1[PER:], c2[PER:], c3z, a, c1[:PER], c2[:PER], c3a)
    pieces = lambda r, q: (r[BLOCK:], r[:BLOCK], q[BLOCK:], q[:BLOCK])
    s0, s1, s2 = swap(r0), swap(r1), swap(r2)
    carried = scores(0, (*pieces(r0, s0), *pieces(r1, s1)), columns)
    r3z, r3b, carried = lax.optimization_barrier((r3z, r3b, carried))
    carried = scores(2, pieces(r2, s2), carried=carried)
    e, zr, partners, sums = scores(3, (r3z, r3b, swap(r3z), swap(r3b)), carried=carried)
    sums = lax.all_to_all(sums, ALL, 0, 0, tiled=True)
    e, zr, partners = (pltpu.with_memory_space_constraint(v, pltpu.HBM) for v in (e, zr, partners))
    here, *away, uc, ur, logs = gradients((4, 5, 6, 7), sums, e, zr, partners)
    other = sum(over_y(*away), here)
    away = gradients((1, 2, 3), logs, e, zr, partners, (uc, ur))
    logs, other = lax.optimization_barrier((logs, other))
    (here,) = gradients((0,), logs, e, zr, partners, (uc, ur))
    mean_objective, grad = finish(z, here, *over_y(*away), lax.ppermute(other, "zl", SWAP))
    return mean_objective[0, 0], grad


def solution(mesh):
    fine = Mesh(mesh.devices.reshape(4, 2, 4, 2, 2), ALL)
    placed = (P(ALL, None), P(ALL))
    return jax.shard_map(
        shards, mesh=fine, in_specs=placed, out_specs=(P(), P(ALL, None)), check_vma=False
    )
```
